512 devices in a mesh: dp: 32 (over y, x, core), group: 2 (over z_hi), tensor: 8 (over z_lo).
Axes of the slice: x: 4, y: 4, z: 16 (z_hi: 2, z_lo: 8; z = z_hi * 8 + z_lo), core: 2. Of those that a mesh axis runs over, the one named last changes fastest.
Arguments:
- teacher_hidden: bfloat16 [256, 4608], P('dp', ('group', 'tensor')), may hold values from -6 to 6
- student_hidden: bfloat16 [256, 3584], P('dp', ('group', 'tensor')), may hold values from -6 to 6
- teacher_gain: bfloat16 [4608], replicated, may hold values from 0.099609375 to 1.8984375
- student_gain: bfloat16 [3584], replicated, may hold values from 0.099609375 to 1.8984375
- teacher_unembed: bfloat16 [131072, 4608], P(('dp', 'group', 'tensor')), may hold values from -0.25 to 0.25
- student_unembed: bfloat16 [131072, 3584], P(('dp', 'group', 'tensor')), may hold values from -0.3125 to 0.3125
- labels: int32 [256], replicated, may hold values from 0 to 131071
Outputs:
- token_loss: float32 [256], P('dp')
- student_grad: bfloat16 [256, 3584], P('dp', ('group', 'tensor'))
The draws below stay inside these ranges and needn't reach their ends.
All inputs are finite; a program needn't handle non-finite values.
Results may differ from the reference program's by a relative error of at most 0.0055.
Values may be sent and summed in bfloat16 or wider, within the bound.
A program may use at most 64 MiB of HBM per device.

```python
import jax
import jax.numpy as jnp
from jax import lax

DT = 4608
DS = 3584
TOKENS = 256
VOCAB = 131072


def place_ends(array, own_key, least, top_value):
    longest = array.shape.index(max(array.shape))
    spots = []
    for shift in (0, 1):
        where = [jax.random.randint(jax.random.fold_in(own_key, axis), (), 0, length) for axis, length in enumerate(array.shape)]
        where[longest] = (where[longest] + shift) % array.shape[longest]
        spots.append(tuple(where))
    return array.at[spots[0]].set(least).at[spots[1]].set(top_value)


def block_scale(rng, extent, cuts, smallest, top_value):
    level = 1.0
    for dim, blocks in cuts:
        draws = jax.random.uniform(jax.random.fold_in(jax.random.fold_in(rng, 6), dim), (blocks,), jnp.float32, smallest / len(cuts), top_value / len(cuts))
        level = level * jnp.repeat(jnp.exp(draws), extent[dim] // blocks).reshape((-1,) + (1,) * (len(extent) - 1 - dim))
    return level


def gaussian(own_key, extent, deviation, limit, split=(), kind=jnp.bfloat16):
    result = deviation * jax.random.normal(own_key, extent, jnp.float32)
    if split:
        result = result * block_scale(own_key, extent, split, -0.22, 0.18)
    return jnp.clip(result, -limit, limit).astype(kind)


def setup_inputs(seed: int = 0) -> dict:
    key_of = jax.random.split(jax.random.key(seed), 8)
    teacher_hidden = gaussian(key_of[0], (TOKENS, DT), 1.0, 6.0, ((0, 32), (1, 16)))
    student_hidden = gaussian(key_of[1], (TOKENS, DS), 1.0, 6.0, ((0, 32), (1, 16)))
    teacher_gain = jnp.clip(1.0 + 0.18 * jax.random.normal(key_of[2], (DT,), jnp.float32), 0.099609375, 1.8984375).astype(jnp.bfloat16)
    student_gain = jnp.clip(1.0 + 0.18 * jax.random.normal(key_of[3], (DS,), jnp.float32), 0.099609375, 1.8984375).astype(jnp.bfloat16)
    teacher_unembed = gaussian(key_of[4], (VOCAB, DT), (DT // 9) ** -0.5, 0.25, ((0, 512),))
    student_unembed = gaussian(key_of[5], (VOCAB, DS), (DS // 9) ** -0.5, 0.3125, ((0, 512),))
    labels = place_ends(jax.random.randint(key_of[6], (TOKENS,), 0, VOCAB), jax.random.fold_in(key_of[6], 1), 0, VOCAB - 1).astype(jnp.int32)
    return dict(teacher_hidden=teacher_hidden, student_hidden=student_hidden, teacher_gain=teacher_gain, student_gain=student_gain, teacher_unembed=teacher_unembed, student_unembed=student_unembed, labels=labels)


SOFT_CAP = 30.0
EPSILON = 1e-06

def normalize(hidden, gain_vector):
    values = hidden.astype(jnp.float32)
    inverse = lax.rsqrt(lax.optimization_barrier(jnp.mean(values * values, axis=1)) + EPSILON)
    scaled = (values * inverse[:, None] * gain_vector.astype(jnp.float32)).astype(jnp.bfloat16)
    return (scaled, inverse)

def reference(teacher_hidden, student_hidden, teacher_gain, student_gain, teacher_unembed, student_unembed, labels):
    scaled_teacher, inv_teacher = normalize(teacher_hidden, teacher_gain)
    scaled_student, inv_student = normalize(student_hidden, student_gain)
    dims = (((1,), (1,)), ((), ()))
    raw_teacher = lax.dot_general(scaled_teacher, teacher_unembed, dims, preferred_element_type=jnp.float32)
    raw_student = lax.dot_general(scaled_student, student_unembed, dims, preferred_element_type=jnp.float32)
    logit_teacher = SOFT_CAP * jnp.tanh(raw_teacher / SOFT_CAP)
    logit_student = SOFT_CAP * jnp.tanh(raw_student / SOFT_CAP)
    exp_teacher = jnp.exp(logit_teacher)
    exp_student = jnp.exp(logit_student)
    vocab_ids = jnp.arange(VOCAB, dtype=jnp.int32)
    onehot = labels[:, None] == vocab_ids[None, :]
    sum_teacher = lax.optimization_barrier(jnp.sum(exp_teacher, axis=1))
    sum_student = lax.optimization_barrier(jnp.sum(exp_student, axis=1))
    cross = lax.optimization_barrier(jnp.sum(exp_teacher * (logit_teacher - logit_student), axis=1))
    picked = lax.optimization_barrier(jnp.sum(jnp.where(onehot, logit_student, 0.0), axis=1))
    token_loss = cross / sum_teacher - jnp.log(sum_teacher) + 2.0 * jnp.log(sum_student) - picked
    slope = 1.0 - (logit_student / SOFT_CAP) ** 2
    grad_logits = (2.0 * exp_student / sum_student[:, None] - exp_teacher / sum_teacher[:, None] - onehot.astype(jnp.float32)) * slope
    grad_round = grad_logits.astype(jnp.bfloat16)
    radial = lax.optimization_barrier(jnp.sum(grad_logits * raw_student, axis=1))
    back = jnp.dot(grad_round, student_unembed, preferred_element_type=jnp.float32)
    values = student_hidden.astype(jnp.float32)
    gain_values = student_gain.astype(jnp.float32)
    student_grad = inv_student[:, None] * gain_values[None, :] * back - (inv_student * inv_student * radial)[:, None] * values / DS
    return (token_loss, student_grad.astype(jnp.bfloat16))
```

```python
import jax
import jax.numpy as jnp
from jax import lax
from jax.experimental import pallas as pl
from jax.experimental.pallas import tpu as pltpu
from jax.sharding import PartitionSpec as P

CAP = 30.0
EPS = 1e-06
MESH = pl.DeviceIdType.MESH
F32 = jnp.float32
BF16 = jnp.bfloat16
RX, RY, RZ = 4, 4, 16
PLANE = RX * RY
NT = (((1,), (1,)), ((), ()))


def kernel(
    th_ref, sh_ref, tg_ref, sg_ref, lab_ref, wt_hbm, ws_hbm,
    grad_ref, loss_ref,
    wt, ws, zbuf, t0, t1, s0, s1, xt, xs, raw_t, raw_s, es_s, et_s, oh_s,
    sxy, sz, gbuf, obuf, rbuf, zsend, zrecv, cols,
    w_send, w_recv, w_loc, z_send, z_recv, g_send, g_recv,
    a_send, a_recv, b_send, b_recv, r_send, r_recv, q_send, q_recv,
):
    dp = lax.axis_index("dp")
    z = lax.axis_index("group") * 8 + lax.axis_index("tensor")
    core = dp % 2
    p = dp // 2
    x = p % RX
    y = p // RX
    tl = th_ref.shape[1]
    sl = sh_ref.shape[1]
    dt = tl * RZ
    ds = sl * RZ
    vloc = wt_hbm.shape[0]

    def at_plane(q):
        return (q * 2 + core, lax.axis_index("group"), lax.axis_index("tensor"))

    def at_line(k):
        return (dp, k // 8, k % 8)

    partner = (p * 2 + 1 - core, lax.axis_index("group"), lax.axis_index("tensor"))

    def remote(src, dst, send, recv, device):
        return pltpu.make_async_remote_copy(
            src_ref=src, dst_ref=dst, send_sem=send, recv_sem=recv,
            device_id=device, device_id_type=MESH,
        )

    own = jnp.concatenate(
        [th_ref[...].astype(F32), sh_ref[...].astype(F32)], axis=1
    )
    zbuf[z] = own.astype(BF16)

    barrier = pltpu.get_barrier_semaphore()

    @pl.loop(1, RZ)
    def _(k):
        pl.semaphore_signal(
            barrier, inc=1, device_id=at_line((z + k) % RZ), device_id_type=MESH
        )
        pl.semaphore_signal(
            barrier, inc=1, device_id=at_plane((p + k) % PLANE), device_id_type=MESH
        )

    pl.semaphore_signal(barrier, inc=1, device_id=partner, device_id_type=MESH)
    pl.semaphore_wait(barrier, 31)

    def z_copy(k, slot):
        return remote(
            zbuf.at[z], zbuf.at[slot], z_send.at[k], z_recv.at[slot],
            at_line((z + k) % RZ),
        )

    @pl.loop(1, RZ)
    def _(k):
        z_copy(k, z).start()

    w_copies = [
        remote(wt_hbm, wt.at[core], w_send.at[0], w_recv.at[0], partner),
        remote(ws_hbm, ws.at[core], w_send.at[1], w_recv.at[1], partner),
    ]
    l_copies = [
        pltpu.make_async_copy(wt_hbm, wt.at[core], w_loc.at[0]),
        pltpu.make_async_copy(ws_hbm, ws.at[core], w_loc.at[1]),
    ]
    for copy in w_copies + l_copies:
        copy.start()

    lane = lax.broadcasted_iota(jnp.int32, (8, 128), 1)
    label_row = jnp.zeros((8, 128), jnp.int32)
    for q in range(PLANE):
        row = jnp.broadcast_to(lab_ref[q // 8 : q // 8 + 1, :], (8, 128))
        shift = (8 * q - 16 * (q % 8) - 8 * core + 256) % 128
        label_row = jnp.where(lane // 8 == q, pltpu.roll(row, shift, 1), label_row)
    labels = label_row[:1, :]

    @pl.loop(1, RZ)
    def _(k):
        z_copy(k, (z + k) % RZ).wait_recv()

    pieces = [zbuf[k].astype(F32) for k in range(RZ)]
    full_t = jnp.concatenate([v[:, :tl] for v in pieces], axis=1)
    full_s = jnp.concatenate([v[:, tl:] for v in pieces], axis=1)

    def scaled(values, gain):
        inv = lax.rsqrt(jnp.sum(values * values, axis=1, keepdims=True) / values.shape[1] + EPS)
        return values * inv * gain, inv

    gain_s = sg_ref[...].astype(F32)
    sc_t, _ = scaled(full_t, tg_ref[...].astype(F32))
    sc_s, inv_s = scaled(full_s, gain_s)
    t0[p] = sc_t[:, : dt // 2].astype(BF16)
    t1[p] = sc_t[:, dt // 2 :].astype(BF16)
    s0[p] = sc_s[:, : ds // 2].astype(BF16)
    s1[p] = sc_s[:, ds // 2 :].astype(BF16)

    def make_ring(c, buf, x_first, forward):
        me1, me2 = (x, y) if x_first else (y, x)

        def slot(i1, i2):
            return i2 * RX + i1 if x_first else i1 * RX + i2

        def send(n, src, axis, step):
            i1, i2 = me1, me2
            if axis == 1:
                i1 = (me1 + step) % 4
            else:
                i2 = (me2 + step) % 4
            remote(
                buf.at[src], buf.at[src], g_send.at[c, n], g_recv.at[c, src],
                at_plane(slot(i1, i2)),
            ).start()

        def recv(src):
            remote(
                buf.at[src], buf.at[src], g_send.at[c, 0], g_recv.at[c, src],
                at_plane(p),
            ).wait_recv()

        def src(o1, o2):
            return slot((me1 + o1 + 4) % 4, (me2 + o2 + 4) % 4)

        return send, recv, src, forward

    rings = [
        make_ring(0, t0, True, 1), make_ring(1, s0, True, -1),
        make_ring(2, t1, False, 1), make_ring(3, s1, False, -1),
    ]
    for send, recv, src, f in rings:
        send(0, src(0, 0), 1, 1)
        send(1, src(0, 0), 1, -1)
    for send, recv, src, f in rings:
        send(2, src(0, 0), 2, 1)
        send(3, src(0, 0), 2, -1)
    for send, recv, src, f in rings:
        recv(src(-f, 0))
        send(4, src(-f, 0), 1, f)
        send(5, src(-f, 0), 2, 1)
        send(6, src(-f, 0), 2, -1)
        recv(src(f, 0))
        send(7, src(f, 0), 2, 1)
        send(8, src(f, 0), 2, -1)
    for send, recv, src, f in rings:
        recv(src(0, -f))
        send(9, src(0, -f), 2, f)
    for send, recv, src, f in rings:
        recv(src(2, 0))
        send(10, src(2, 0), 2, 1)
        send(11, src(2, 0), 2, -1)
    for n, o in ((12, -1), (13, 1), (14, 2)):
        for send, recv, src, f in rings:
            recv(src(o, -f))
            send(n, src(o, -f), 2, f)
    for o in (0, -1, 1, 2):
        for send, recv, src, f in rings:
            recv(src(o, f))
            recv(src(o, 2))

    for copy in l_copies:
        copy.wait()
    for copy in w_copies:
        copy.wait()

    def rows_of(buf):
        return buf[...].astype(F32).reshape(PLANE * 8, buf.shape[2]).astype(BF16)

    xt[:, : dt // 2] = rows_of(t0)
    xt[:, dt // 2 :] = rows_of(t1)
    xs[:, : ds // 2] = rows_of(s0)
    xs[:, ds // 2 :] = rows_of(s1)
    sums = [jnp.zeros((1, 128), F32) for _ in range(7)]
    for half in range(2):
        raw_t[...] = lax.dot_general(wt[half], xt[...], NT, preferred_element_type=F32)
        raw_s[...] = lax.dot_general(ws[half], xs[...], NT, preferred_element_type=F32)
        vocab0 = ((p * 2 + half) * RZ + z) * vloc
        ids = vocab0 + lax.broadcasted_iota(jnp.int32, (vloc, 128), 0)
        onehot = ids == labels
        rs = raw_s[...]
        tan_t = jnp.tanh(raw_t[...] * (1.0 / CAP))
        tan_s = jnp.tanh(rs * (1.0 / CAP))
        log_t = CAP * tan_t
        log_s = CAP * tan_s
        exp_t = jnp.exp(log_t)
        exp_s = jnp.exp(log_s)
        slope = 1.0 - tan_s * tan_s
        e_s = exp_s * slope
        e_t = exp_t * slope
        o_h = jnp.where(onehot, slope, 0.0)
        es_s[half] = e_s
        et_s[half] = e_t
        oh_s[half] = o_h
        terms = (
            exp_t, exp_s, exp_t * (log_t - log_s), jnp.where(onehot, log_s, 0.0),
            e_s * rs, e_t * rs, o_h * rs,
        )
        sums = [a + jnp.sum(v, axis=0, keepdims=True) for a, v in zip(sums, terms)]

    sxy[p] = jnp.concatenate(sums + [jnp.zeros((1, 128), F32)], axis=0)

    def a_copy(k, slot):
        return remote(
            sxy.at[p], sxy.at[slot], a_send.at[k], a_recv.at[slot],
            at_plane((p + k) % PLANE),
        )

    def b_copy(k, slot):
        return remote(
            sz.at[z], sz.at[slot], b_send.at[k], b_recv.at[slot],
            at_line((z + k) % RZ),
        )

    @pl.loop(1, PLANE)
    def _(k):
        a_copy(k, p).start()

    @pl.loop(1, PLANE)
    def _(k):
        a_copy(k, (p + k) % PLANE).wait_recv()

    sz[z] = jnp.sum(sxy[...], axis=0)

    @pl.loop(1, RZ)
    def _(k):
        b_copy(k, z).start()

    @pl.loop(1, RZ)
    def _(k):
        b_copy(k, (z + k) % RZ).wait_recv()

    total = jnp.sum(sz[...], axis=0)
    sum_t, sum_s, cross, picked = (total[i : i + 1] for i in range(4))
    scale_s = 2.0 / sum_s
    scale_t = 1.0 / sum_t

    for half in range(2):
        grad = es_s[half] * scale_s - et_s[half] * scale_t - oh_s[half]
        gbuf[:, half * vloc : (half + 1) * vloc] = grad.T.astype(BF16)
    part = 512
    for n in range(ds // part):
        cut = slice(n * part, (n + 1) * part)
        term = jnp.dot(
            gbuf[:, :vloc], ws[0, :, cut], preferred_element_type=F32
        ) + jnp.dot(gbuf[:, vloc:], ws[1, :, cut], preferred_element_type=F32)
        obuf[:, :, cut] = term.reshape(PLANE, 8, part).astype(BF16)

    def r_copy(k, src, slot):
        return remote(
            obuf.at[src], rbuf.at[slot], r_send.at[k], r_recv.at[slot],
            at_plane((p + k) % PLANE),
        )

    @pl.loop(1, PLANE)
    def _(k):
        r_copy(k, (p + k) % PLANE, p).start()

    loss = cross / sum_t - jnp.log(sum_t) + 2.0 * jnp.log(sum_s) - picked
    radial = scale_s * total[4:5] - scale_t * total[5:6] - total[6:7]
    packed = jnp.concatenate([loss, radial, jnp.zeros((6, 128), F32)], axis=0)
    cols[...] = packed.T
    mine = cols[pl.ds(p * 8, 8), :]
    loss_ref[...] = mine[:, :1]
    rad = mine[:, 1:2]

    rbuf[p] = obuf[p]

    @pl.loop(1, PLANE)
    def _(k):
        r_copy(k, (p + k) % PLANE, (p + k) % PLANE).wait_recv()

    back = jnp.sum(rbuf[...].astype(F32), axis=0) * gain_s
    for k in range(RZ):
        zsend[k, :, :sl] = back[:, k * sl : (k + 1) * sl].astype(BF16)

    def q_copy(k, src, slot):
        return remote(
            zsend.at[src], zrecv.at[slot], q_send.at[k], q_recv.at[slot],
            at_line((z + k) % RZ),
        )

    @pl.loop(1, RZ)
    def _(k):
        q_copy(k, (z + k) % RZ, z).start()

    zrecv[z] = zsend[z]

    @pl.loop(1, RZ)
    def _(k):
        q_copy(k, (z + k) % RZ, (z + k) % RZ).wait_recv()

    sum_back = jnp.sum(zrecv[...].astype(F32), axis=0)[:, :sl]
    out = inv_s * sum_back - (inv_s * inv_s * rad) * sh_ref[...].astype(F32) / ds
    grad_ref[...] = out.astype(BF16)

    @pl.loop(1, RZ)
    def _(k):
        z_copy(k, z).wait_send()
        a_copy(k, p).wait_send()
        b_copy(k, z).wait_send()
        r_copy(k, p, p).wait_send()
        q_copy(k, z, z).wait_send()

    for c, buf in enumerate((t0, s0, t1, s1)):
        @pl.loop(0, 15)
        def _(n):
            remote(
                buf.at[p], buf.at[p], g_send.at[c, n], g_recv.at[c, p], at_plane(p)
            ).wait_send()


def on_device(th, sh, tg, sg, wt, ws, labels):
    tok, tl = th.shape
    sl = sh.shape[1]
    dt, ds, vloc = tl * RZ, sl * RZ, wt.shape[0]
    vmem = pl.BlockSpec(memory_space=pltpu.VMEM)
    hbm = pl.BlockSpec(memory_space=pl.ANY)
    dma = pltpu.SemaphoreType.DMA
    grad, loss = pl.pallas_call(
        kernel,
        out_shape=(
            jax.ShapeDtypeStruct((tok, sl), BF16),
            jax.ShapeDtypeStruct((tok, 1), F32),
        ),
        in_specs=[vmem] * 5 + [hbm] * 2,
        out_specs=(vmem, vmem),
        scratch_shapes=[
            pltpu.VMEM((2, vloc, dt), BF16),
            pltpu.VMEM((2, vloc, ds), BF16),
            pltpu.VMEM((RZ, tok, tl + sl), BF16),
            pltpu.VMEM((PLANE, tok, dt // 2), BF16),
            pltpu.VMEM((PLANE, tok, dt // 2), BF16),
            pltpu.VMEM((PLANE, tok, ds // 2), BF16),
            pltpu.VMEM((PLANE, tok, ds // 2), BF16),
            pltpu.VMEM((128, dt), BF16),
            pltpu.VMEM((128, ds), BF16),
            pltpu.VMEM((vloc, 128), F32),
            pltpu.VMEM((vloc, 128), F32),
            pltpu.VMEM((2, vloc, 128), F32),
            pltpu.VMEM((2, vloc, 128), F32),
            pltpu.VMEM((2, vloc, 128), F32),
            pltpu.VMEM((PLANE, 8, 128), F32),
            pltpu.VMEM((RZ, 8, 128), F32),
            pltpu.VMEM((128, 2 * vloc), BF16),
            pltpu.VMEM((PLANE, tok, ds), BF16),
            pltpu.VMEM((PLANE, tok, ds), BF16),
            pltpu.VMEM((RZ, tok, 256), BF16),
            pltpu.VMEM((RZ, tok, 256), BF16),
            pltpu.VMEM((128, 8), F32),
            dma((2,)), dma((2,)), dma((2,)),
            dma((RZ,)), dma((RZ,)),
            dma((4, 15)), dma((4, PLANE)),
            dma((PLANE,)), dma((PLANE,)),
            dma((RZ,)), dma((RZ,)),
            dma((PLANE,)), dma((PLANE,)),
            dma((RZ,)), dma((RZ,)),
        ],
        compiler_params=pltpu.CompilerParams(
            collective_id=0, has_side_effects=True, vmem_limit_bytes=56 * 1024 * 1024
        ),
    )(th, sh, tg.reshape(1, dt), sg.reshape(1, ds), labels.reshape(2, 128), wt, ws)
    return (loss.reshape(tok), grad)


def solution(mesh):
    in_specs = (
        P("dp", ("group", "tensor")),
        P("dp", ("group", "tensor")),
        P(),
        P(),
        P(("dp", "group", "tensor"), None),
        P(("dp", "group", "tensor"), None),
        P(),
    )
    out_specs = (P("dp"), P("dp", ("group", "tensor")))
    return jax.shard_map(
        on_device, mesh=mesh, in_specs=in_specs, out_specs=out_specs, check_vma=False
    )
```

```python
import jax
import jax.numpy as jnp
from jax import lax
from jax.experimental import pallas as pl
from jax.experimental.pallas import tpu as pltpu
from jax.sharding import PartitionSpec as P

CAP = 30.0
EPS = 1e-06
MESH = pl.DeviceIdType.MESH
F32 = jnp.float32
BF16 = jnp.bfloat16
RX, RY, RZ = 4, 4, 16
PLANE = RX * RY
NT = (((1,), (1,)), ((), ()))


def kernel(
    th_ref, sh_ref, tg_ref, sg_ref, lab_ref, wt_hbm, ws_hbm,
    out_ref,
    wt, ws, buf, ibuf, gt, gs, raw_t, raw_s, es_s, et_s, oh_s,
    sxy, sz, gbuf, obuf, rbuf, zsend, zrecv, cols,
    w_send, w_recv, w_loc, z_send, z_recv, g_send, g_recv, i_send, i_recv,
    a_send, a_recv, b_send, b_recv, r_send, r_recv, q_send, q_recv,
):
    dp = lax.axis_index("dp")
    z = lax.axis_index("group") * 8 + lax.axis_index("tensor")
    core = dp % 2
    p = dp // 2
    x = p % RX
    y = p // RX
    quad = z // 4
    tl = th_ref.shape[1]
    sl = sh_ref.shape[1]
    ds = sl * RZ
    vloc = wt_hbm.shape[0]

    def at_plane(q):
        return (q * 2 + core, lax.axis_index("group"), lax.axis_index("tensor"))

    def at_line(k):
        return (dp, k // 8, k % 8)

    partner = (p * 2 + 1 - core, lax.axis_index("group"), lax.axis_index("tensor"))

    def remote(src, dst, send, recv, device):
        return pltpu.make_async_remote_copy(
            src_ref=src, dst_ref=dst, send_sem=send, recv_sem=recv,
            device_id=device, device_id_type=MESH,
        )

    barrier = pltpu.get_barrier_semaphore()

    @pl.loop(1, RZ)
    def _(k):
        pl.semaphore_signal(
            barrier, inc=1, device_id=at_line((z + k) % RZ), device_id_type=MESH
        )
        pl.semaphore_signal(
            barrier, inc=1, device_id=at_plane((p + k) % PLANE), device_id_type=MESH
        )

    pl.semaphore_signal(barrier, inc=1, device_id=partner, device_id_type=MESH)

    l_copies = [
        pltpu.make_async_copy(wt_hbm, wt.at[core], w_loc.at[0]),
        pltpu.make_async_copy(ws_hbm, ws.at[core], w_loc.at[1]),
    ]
    for copy in l_copies:
        copy.start()

    own = jnp.concatenate(
        [th_ref[...].astype(F32), sh_ref[...].astype(F32)], axis=1
    )
    buf[quad, p, z % 4] = own.astype(BF16)

    for gain_ref, wide in ((tg_ref, gt), (sg_ref, gs)):
        gain = gain_ref[...].astype(F32)
        for i in range(gain.shape[0]):
            wide[:, i * 128 : (i + 1) * 128] = gain[i : i + 1]

    lane = lax.broadcasted_iota(jnp.int32, (8, 128), 1)
    label_row = jnp.zeros((8, 128), jnp.int32)
    for q in range(PLANE):
        row = jnp.broadcast_to(lab_ref[q // 8 : q // 8 + 1, :], (8, 128))
        shift = (8 * q - 16 * (q % 8) - 8 * core + 256) % 128
        label_row = jnp.where(lane // 8 == q, pltpu.roll(row, shift, 1), label_row)
    labels = label_row[:1, :]

    pl.semaphore_wait(barrier, 31)

    def await_recv(ref, sem):
        remote(ref, ref, w_send.at[0], sem, partner).wait_recv()

    def await_send(ref, sem):
        remote(ref, ref, sem, w_recv.at[0], partner).wait_send()

    slab = buf.at[quad, p, z % 4]

    def z_start(k):
        to = (z + k + RZ) % RZ
        remote(
            slab, slab, z_send.at[0], z_recv.at[(quad - to // 4 + 4) % 4], at_line(to)
        ).start()

    @pl.loop(1, 8)
    def _(k):
        z_start(k)
        z_start(-k)

    z_start(8)

    w_copies = [
        remote(wt_hbm, wt.at[core], w_send.at[0], w_recv.at[0], partner),
        remote(ws_hbm, ws.at[core], w_send.at[1], w_recv.at[1], partner),
    ]
    for copy in w_copies:
        copy.start()

    class Ring:
        def __init__(self, c, delta, x_first):
            self.c, self.q, self.delta = c, (quad + delta) % 4, delta
            self.x_first = x_first
            self.me1, self.me2 = (x, y) if x_first else (y, x)

        def src(self, o1, o2):
            i1, i2 = (self.me1 + o1 + 4) % 4, (self.me2 + o2 + 4) % 4
            return i2 * RX + i1 if self.x_first else i1 * RX + i2

        def send(self, o1, to1, to2, sem):
            ref = buf.at[self.q, self.src(o1, 0)]
            remote(
                ref, ref, g_send.at[self.c], g_recv.at[self.c, sem],
                at_plane(self.src(to1, to2)),
            ).start()

        def begin(self):
            n = 3 if self.delta == 0 else 4
            await_recv(buf.at[self.q, p, pl.ds(0, n)], z_recv.at[self.delta])
            for o in (1, -1, 2):
                self.send(0, o, 0, o + 1)
            for o in (1, -1, 2):
                self.send(0, 0, o, 1)

        def middle(self):
            for o in (-1, 1, 2):
                await_recv(buf.at[self.q, p], g_recv.at[self.c, {-1: 2, 1: 0, 2: 3}[o]])
                for to in (1, -1, 2):
                    self.send(o, 0, to, 1)

        def finish(self):
            await_recv(buf.at[self.q, pl.ds(0, 12)], g_recv.at[self.c, 1])

    r0, r1, r2, r3 = rings = [
        Ring(0, 0, True), Ring(1, 1, False), Ring(2, 3, True), Ring(3, 2, False)
    ]
    r0.begin()
    r1.begin()
    r2.begin()
    r0.middle()
    r3.begin()
    squares = jnp.zeros((8, tl + sl), F32)
    for k in range(4):
        for j in range(4):
            v = buf[k, p, j].astype(F32)
            squares = squares + v * v
    own_t = jnp.sum(squares[:, :tl], axis=1, keepdims=True)
    own_s = jnp.sum(squares[:, tl:], axis=1, keepdims=True)
    inv_t = lax.rsqrt(own_t / (tl * RZ) + EPS)
    inv_s = lax.rsqrt(own_s / ds + EPS)
    ibuf[p] = jnp.where(lane == 0, inv_t, inv_s)

    def i_copy(k):
        return remote(
            ibuf.at[p], ibuf.at[p], i_send.at[0], i_recv.at[0],
            at_plane((p + k) % PLANE),
        )

    @pl.loop(1, PLANE)
    def _(k):
        i_copy(k).start()

    r1.middle()
    r2.middle()
    r3.middle()
    await_recv(ibuf.at[pl.ds(0, PLANE - 1)], i_recv.at[0])
    for copy in l_copies:
        copy.wait()
    for copy in w_copies:
        copy.wait()

    all_t = ibuf[:, :, 0:1].reshape(PLANE * 8, 1)
    all_s = ibuf[:, :, 1:2].reshape(PLANE * 8, 1)

    def multiply(ring):
        pieces = [
            buf[ring.q, :, j].astype(F32).reshape(PLANE * 8, tl + sl) for j in range(4)
        ]
        cut_t = pl.ds(pl.multiple_of(ring.q * (4 * tl), 128), 4 * tl)
        cut_s = pl.ds(pl.multiple_of(ring.q * (4 * sl), 128), 4 * sl)
        v_t = jnp.concatenate([v[:, :tl] for v in pieces], axis=1)
        v_s = jnp.concatenate([v[:, tl:] for v in pieces], axis=1)
        x_t = (v_t * all_t * gt[:, cut_t]).astype(BF16)
        x_s = (v_s * all_s * gs[:, cut_s]).astype(BF16)
        for half in range(2):
            d_t = lax.dot_general(wt[half, :, cut_t], x_t, NT, preferred_element_type=F32)
            d_s = lax.dot_general(ws[half, :, cut_s], x_s, NT, preferred_element_type=F32)
            if ring.c == 0:
                raw_t[half] = d_t
                raw_s[half] = d_s
            else:
                raw_t[half] += d_t
                raw_s[half] += d_s

    r0.finish()
    multiply(r0)
    r1.finish()
    multiply(r1)
    r2.finish()
    multiply(r2)
    r3.finish()
    multiply(r3)

    sums = [jnp.zeros((1, 128), F32) for _ in range(7)]
    for half in range(2):
        vocab0 = ((p * 2 + half) * RZ + z) * vloc
        ids = vocab0 + lax.broadcasted_iota(jnp.int32, (vloc, 128), 0)
        onehot = ids == labels
        rs = raw_s[half]
        tan_t = jnp.tanh(raw_t[half] * (1.0 / CAP))
        tan_s = jnp.tanh(rs * (1.0 / CAP))
        log_t = CAP * tan_t
        log_s = CAP * tan_s
        exp_t = jnp.exp(log_t)
        exp_s = jnp.exp(log_s)
        slope = 1.0 - tan_s * tan_s
        e_s = exp_s * slope
        e_t = exp_t * slope
        o_h = jnp.where(onehot, slope, 0.0)
        es_s[half] = e_s
        et_s[half] = e_t
        oh_s[half] = o_h
        terms = (
            exp_t, exp_s, exp_t * (log_t - log_s), jnp.where(onehot, log_s, 0.0),
            e_s * rs, e_t * rs, o_h * rs,
        )
        sums = [a + jnp.sum(v, axis=0, keepdims=True) for a, v in zip(sums, terms)]

    sxy[p] = jnp.concatenate(sums + [jnp.zeros((1, 128), F32)], axis=0)

    def a_copy(k):
        return remote(
            sxy.at[p], sxy.at[p], a_send.at[0], a_recv.at[0],
            at_plane((p + k) % PLANE),
        )

    def b_copy(k):
        return remote(
            sz.at[z], sz.at[z], b_send.at[0], b_recv.at[0],
            at_line((z + k) % RZ),
        )

    @pl.loop(1, PLANE)
    def _(k):
        a_copy(k).start()

    await_recv(sxy.at[pl.ds(0, PLANE - 1)], a_recv.at[0])

    sz[z] = jnp.sum(sxy[...], axis=0)

    @pl.loop(1, RZ)
    def _(k):
        b_copy(k).start()

    await_recv(sz.at[pl.ds(0, RZ - 1)], b_recv.at[0])

    total = jnp.sum(sz[...], axis=0)
    sum_t, sum_s, cross, picked = (total[i : i + 1] for i in range(4))
    scale_s = 2.0 / sum_s
    scale_t = 1.0 / sum_t

    for half in range(2):
        grad = es_s[half] * scale_s - et_s[half] * scale_t - oh_s[half]
        gbuf[:, half * vloc : (half + 1) * vloc] = grad.T.astype(BF16)
    part = 512
    for n in range(ds // part):
        cut = slice(n * part, (n + 1) * part)
        term = jnp.dot(
            gbuf[:, :vloc], ws[0, :, cut], preferred_element_type=F32
        ) + jnp.dot(gbuf[:, vloc:], ws[1, :, cut], preferred_element_type=F32)
        obuf[:, :, cut] = term.reshape(PLANE, 8, part).astype(BF16)

    def r_copy(k):
        to = (p + k) % PLANE
        return remote(
            obuf.at[to], rbuf.at[p], r_send.at[0], r_recv.at[0], at_plane(to)
        )

    @pl.loop(1, PLANE)
    def _(k):
        r_copy(k).start()

    loss = cross / sum_t - jnp.log(sum_t) + 2.0 * jnp.log(sum_s) - picked
    radial = scale_s * total[4:5] - scale_t * total[5:6] - total[6:7]
    packed = jnp.concatenate([loss, radial, jnp.zeros((6, 128), F32)], axis=0)
    cols[...] = packed.T
    mine = cols[pl.ds(p * 8, 8), :]
    out_ref[:, 256:] = jnp.broadcast_to(mine[:, :1], (8, 128))
    rad = mine[:, 1:2]

    rbuf[p] = obuf[p]

    await_recv(rbuf.at[pl.ds(0, PLANE - 1)], r_recv.at[0])

    back = jnp.sum(rbuf[...].astype(F32), axis=0) * gs[...]
    for k in range(RZ):
        zsend[k, :, :sl] = back[:, k * sl : (k + 1) * sl].astype(BF16)

    def q_copy(k):
        to = (z + k) % RZ
        return remote(
            zsend.at[to], zrecv.at[z], q_send.at[0], q_recv.at[0], at_line(to)
        )

    @pl.loop(1, RZ)
    def _(k):
        q_copy(k).start()

    await_send(buf.at[0, pl.ds(0, RZ - 1), 0], z_send.at[0])
    await_send(ibuf.at[pl.ds(0, PLANE - 1)], i_send.at[0])
    await_send(sxy.at[pl.ds(0, PLANE - 1)], a_send.at[0])
    await_send(sz.at[pl.ds(0, RZ - 1)], b_send.at[0])
    for ring in rings:
        await_send(buf.at[ring.q, pl.ds(0, 15)], g_send.at[ring.c])

    zrecv[z] = zsend[z]

    await_recv(zrecv.at[pl.ds(0, RZ - 1)], q_recv.at[0])

    sum_back = jnp.sum(zrecv[...].astype(F32), axis=0)[:, :sl]
    out = inv_s * sum_back - (inv_s * inv_s * rad) * sh_ref[...].astype(F32) / ds
    out_ref[:, :sl] = out

    await_send(obuf.at[pl.ds(0, PLANE - 1)], r_send.at[0])
    await_send(zsend.at[pl.ds(0, RZ - 1)], q_send.at[0])


def on_device(th, sh, tg, sg, wt, ws, labels):
    tok, tl = th.shape
    sl = sh.shape[1]
    dt, ds, vloc = tl * RZ, sl * RZ, wt.shape[0]
    vmem = pl.BlockSpec(memory_space=pltpu.VMEM)
    hbm = pl.BlockSpec(memory_space=pl.ANY)
    dma = pltpu.SemaphoreType.DMA
    out = pl.pallas_call(
        kernel,
        out_shape=jax.ShapeDtypeStruct((tok, 384), F32),
        in_specs=[vmem] * 5 + [hbm] * 2,
        out_specs=vmem,
        scratch_shapes=[
            pltpu.VMEM((2, vloc, dt), BF16),
            pltpu.VMEM((2, vloc, ds), BF16),
            pltpu.VMEM((4, PLANE, 4, tok, tl + sl), BF16),
            pltpu.VMEM((PLANE, tok, 128), F32),
            pltpu.VMEM((1, dt), F32),
            pltpu.VMEM((1, ds), F32),
            pltpu.VMEM((2, vloc, 128), F32),
            pltpu.VMEM((2, vloc, 128), F32),
            pltpu.VMEM((2, vloc, 128), F32),
            pltpu.VMEM((2, vloc, 128), F32),
            pltpu.VMEM((2, vloc, 128), F32),
            pltpu.VMEM((PLANE, 8, 128), F32),
            pltpu.VMEM((RZ, 8, 128), F32),
            pltpu.VMEM((128, 2 * vloc), BF16),
            pltpu.VMEM((PLANE, tok, ds), BF16),
            pltpu.VMEM((PLANE, tok, ds), BF16),
            pltpu.VMEM((RZ, tok, 256), BF16),
            pltpu.VMEM((RZ, tok, 256), BF16),
            pltpu.VMEM((128, 8), F32),
            dma((2,)), dma((2,)), dma((2,)),
            dma((1,)), dma((4,)),
            dma((4,)), dma((4, 4)),
            dma((1,)), dma((1,)),
            dma((1,)), dma((1,)),
            dma((1,)), dma((1,)),
            dma((1,)), dma((1,)),
            dma((1,)), dma((1,)),
        ],
        compiler_params=pltpu.CompilerParams(
            collective_id=0, has_side_effects=True, vmem_limit_bytes=56 * 1024 * 1024
        ),
    )(th, sh, tg.reshape(-1, 128), sg.reshape(-1, 128), labels.reshape(2, 128), wt, ws)
    return (out[:, 256], out[:, :sl].astype(BF16))


def solution(mesh):
    in_specs = (
        P("dp", ("group", "tensor")),
        P("dp", ("group", "tensor")),
        P(),
        P(),
        P(("dp", "group", "tensor"), None),
        P(("dp", "group", "tensor"), None),
        P(),
    )
    out_specs = (P("dp"), P("dp", ("group", "tensor")))
    return jax.shard_map(
        on_device, mesh=mesh, in_specs=in_specs, out_specs=out_specs, check_vma=False
    )
```

```python
import jax
import jax.numpy as jnp
from jax import lax
from jax.experimental import pallas as pl
from jax.experimental.pallas import tpu as pltpu
from jax.sharding import PartitionSpec as P

CAP = 30.0
EPS = 1e-06
MESH = pl.DeviceIdType.MESH
F32 = jnp.float32
BF16 = jnp.bfloat16
RX, RY, RZ = 4, 4, 16
PLANE = RX * RY
NT = (((1,), (1,)), ((), ()))


def kernel(
    th_hbm, sh_hbm, tg_hbm, sg_hbm, lab_hbm, wt_hbm, ws_hbm,
    out_ref,
    th_ref, sh_ref, tg_ref, sg_ref, lab_ref, wt, ws, buf, ibuf, gt, gs, raw_t, raw_s, es_s, et_s, oh_s,
    sxy, sz, gbuf, obuf, rbuf, zsend, zrecv, cols,
    w_send, w_recv, w_loc, s_loc, z_send, z_recv, g_send, g_recv, i_send, i_recv,
    a_send, a_recv, b_send, b_recv, r_send, r_recv, q_send, q_recv,
):
    dp = lax.axis_index("dp")
    z = lax.axis_index("group") * 8 + lax.axis_index("tensor")
    core = dp % 2
    p = dp // 2
    x = p % RX
    y = p // RX
    quad = z // 4
    tl = th_ref.shape[1]
    sl = sh_ref.shape[1]
    ds = sl * RZ
    vloc = wt_hbm.shape[0]

    def at_plane(q):
        return (q * 2 + core, lax.axis_index("group"), lax.axis_index("tensor"))

    def at_line(k):
        return (dp, k // 8, k % 8)

    partner = (p * 2 + 1 - core, lax.axis_index("group"), lax.axis_index("tensor"))

    def remote(src, dst, send, recv, device):
        return pltpu.make_async_remote_copy(
            src_ref=src, dst_ref=dst, send_sem=send, recv_sem=recv,
            device_id=device, device_id_type=MESH,
        )

    small = [
        pltpu.make_async_copy(src, dst, s_loc.at[i])
        for i, (src, dst) in enumerate(
            (
                (th_hbm, th_ref), (sh_hbm, sh_ref), (tg_hbm, tg_ref),
                (sg_hbm, sg_ref), (lab_hbm, lab_ref),
            )
        )
    ]
    for copy in small:
        copy.start()

    barrier = pltpu.get_barrier_semaphore()

    @pl.loop(1, RZ)
    def _(k):
        pl.semaphore_signal(
            barrier, inc=1, device_id=at_line((z + k) % RZ), device_id_type=MESH
        )
        pl.semaphore_signal(
            barrier, inc=1, device_id=at_plane((p + k) % PLANE), device_id_type=MESH
        )

    pl.semaphore_signal(barrier, inc=1, device_id=partner, device_id_type=MESH)

    l_copies = [
        pltpu.make_async_copy(wt_hbm, wt.at[core], w_loc.at[0]),
        pltpu.make_async_copy(ws_hbm, ws.at[core], w_loc.at[1]),
    ]
    for copy in l_copies:
        copy.start()

    for copy in small:
        copy.wait()

    own = jnp.concatenate(
        [th_ref[...].astype(F32), sh_ref[...].astype(F32)], axis=1
    )
    buf[quad, p, z % 4] = own.astype(BF16)

    for gain_ref, wide in ((tg_ref, gt), (sg_ref, gs)):
        gain = gain_ref[...].astype(F32)
        for i in range(gain.shape[0]):
            wide[:, i * 128 : (i + 1) * 128] = gain[i : i + 1]

    lane = lax.broadcasted_iota(jnp.int32, (8, 128), 1)
    label_row = jnp.zeros((8, 128), jnp.int32)
    for q in range(PLANE):
        row = jnp.broadcast_to(lab_ref[q // 8 : q // 8 + 1, :], (8, 128))
        shift = (8 * q - 16 * (q % 8) - 8 * core + 256) % 128
        label_row = jnp.where(lane // 8 == q, pltpu.roll(row, shift, 1), label_row)
    labels = label_row[:1, :]

    pl.semaphore_wait(barrier, 31)

    def await_recv(ref, sem):
        remote(ref, ref, w_send.at[0], sem, partner).wait_recv()

    def await_send(ref, sem):
        remote(ref, ref, sem, w_recv.at[0], partner).wait_send()

    slab = buf.at[quad, p, z % 4]

    def z_start(k):
        to = (z + k + RZ) % RZ
        remote(
            slab, slab, z_send.at[0], z_recv.at[(quad - to // 4 + 4) % 4], at_line(to)
        ).start()

    @pl.loop(1, 8)
    def _(k):
        z_start(k)
        z_start(-k)

    z_start(8)

    w_copies = [
        remote(wt_hbm, wt.at[core], w_send.at[0], w_recv.at[0], partner),
        remote(ws_hbm, ws.at[core], w_send.at[1], w_recv.at[1], partner),
    ]
    for copy in w_copies:
        copy.start()

    class Ring:
        def __init__(self, c, delta, x_first, way):
            self.c, self.q, self.delta = c, (quad + delta) % 4, delta
            self.x_first, self.way = x_first, way
            self.me1, self.me2 = (x, y) if x_first else (y, x)
            self.alone = {
                ("first", 1): 0, ("first", -1): 1, ("far", 0): 2,
                ("second", 0): 3, ("second", -1): 4, ("second", 1): 5, ("second", 2): 6,
            }

        def src(self, o1, o2):
            i1, i2 = (self.me1 + o1 + 4) % 4, (self.me2 + o2 + 4) % 4
            return i2 * RX + i1 if self.x_first else i1 * RX + i2

        def send(self, o1, o2, to1, to2, sem):
            ref = buf.at[self.q, self.src(o1, o2)]
            remote(
                ref, ref, g_send.at[self.c], g_recv.at[self.c, sem],
                at_plane(self.src(to1, to2)),
            ).start()

        def wait(self, sem):
            await_recv(buf.at[self.q, p], g_recv.at[self.c, sem])

        def second(self, o):
            self.send(o, 0, 0, self.way, self.alone["second", o])
            self.send(o, 0, 0, -self.way, 7)

        def begin(self):
            n = 3 if self.c == 0 else 4
            await_recv(buf.at[self.q, p, pl.ds(0, n)], z_recv.at[self.delta])
            for to in (1, -1):
                self.send(0, 0, to, 0, self.alone["first", to])
            self.second(0)

        def near(self):
            way = self.way
            self.wait(self.alone["first", way])
            self.send(-way, 0, way, 0, self.alone["far", 0])
            self.second(-way)
            self.wait(self.alone["first", -way])
            self.second(way)

        def far(self):
            self.wait(self.alone["far", 0])
            self.second(2)

        def column(self, o):
            self.wait(self.alone["second", o])
            self.send(o, -self.way, 0, self.way, 7)

        def finish(self):
            await_recv(buf.at[self.q, pl.ds(0, 8)], g_recv.at[self.c, 7])

    class TwoStep(Ring):
        def begin(self):
            await_recv(buf.at[self.q, p], z_recv.at[self.delta])
            for sem, to in enumerate((1, -1, 2)):
                self.send(0, 0, to, 0, sem)
            for to in (1, -1, 2):
                self.send(0, 0, 0, to, 7)

        def middle(self):
            for sem, o in enumerate((-1, 1, 2)):
                self.wait(sem)
                for to in (1, -1, 2):
                    self.send(o, 0, 0, to, 7)

        def finish(self):
            await_recv(buf.at[self.q, pl.ds(0, 12)], g_recv.at[self.c, 7])


    class TwoStep(Ring):
        def begin(self):
            await_recv(buf.at[self.q, p], z_recv.at[self.delta])
            for sem, to in enumerate((1, -1, 2)):
                self.send(0, 0, to, 0, sem)
            for to in (1, -1, 2):
                self.send(0, 0, 0, to, 7)

        def middle(self):
            for sem, o in enumerate((-1, 1, 2)):
                self.wait(sem)
                for to in (1, -1, 2):
                    self.send(o, 0, 0, to, 7)

        def finish(self):
            await_recv(buf.at[self.q, pl.ds(0, 12)], g_recv.at[self.c, 7])

    beside = jnp.where(z % 4 < 2, 3, 1)
    r0, r1, r2, r3 = rings = [
        Ring(0, 0, True, 1), Ring(1, beside, False, 1),
        Ring(2, 4 - beside, True, -1), TwoStep(3, 2, False, -1),
    ]
    r0.begin()
    r1.begin()
    r0.near()
    r0.column(0)
    r2.begin()
    r1.near()
    r1.column(0)
    r0.far()
    r0.column(-1)
    r0.column(1)
    r3.begin()
    squares = jnp.zeros((8, tl + sl), F32)
    for k in range(4):
        for j in range(4):
            v = buf[k, p, j].astype(F32)
            squares = squares + v * v
    own_t = jnp.sum(squares[:, :tl], axis=1, keepdims=True)
    own_s = jnp.sum(squares[:, tl:], axis=1, keepdims=True)
    inv_t = lax.rsqrt(own_t / (tl * RZ) + EPS)
    inv_s = lax.rsqrt(own_s / ds + EPS)
    ibuf[p] = jnp.where(lane == 0, inv_t, inv_s)

    def i_copy(k):
        return remote(
            ibuf.at[p], ibuf.at[p], i_send.at[0], i_recv.at[0],
            at_plane((p + k) % PLANE),
        )

    @pl.loop(1, PLANE)
    def _(k):
        i_copy(k).start()

    r2.near()
    r2.column(0)
    r1.far()
    r1.column(-1)
    r1.column(1)
    r0.column(2)
    r3.middle()
    r2.far()
    r2.column(-1)
    r2.column(1)
    r1.column(2)
    await_recv(ibuf.at[pl.ds(0, PLANE - 1)], i_recv.at[0])
    for copy in l_copies:
        copy.wait()
    for copy in w_copies:
        copy.wait()

    all_t = ibuf[:, :, 0:1].reshape(PLANE * 8, 1)
    all_s = ibuf[:, :, 1:2].reshape(PLANE * 8, 1)

    def multiply(ring):
        pieces = [
            buf[ring.q, :, j].astype(F32).reshape(PLANE * 8, tl + sl) for j in range(4)
        ]
        cut_t = pl.ds(pl.multiple_of(ring.q * (4 * tl), 128), 4 * tl)
        cut_s = pl.ds(pl.multiple_of(ring.q * (4 * sl), 128), 4 * sl)
        v_t = jnp.concatenate([v[:, :tl] for v in pieces], axis=1)
        v_s = jnp.concatenate([v[:, tl:] for v in pieces], axis=1)
        x_t = (v_t * all_t * gt[:, cut_t]).astype(BF16)
        x_s = (v_s * all_s * gs[:, cut_s]).astype(BF16)
        for half in range(2):
            d_t = lax.dot_general(wt[half, :, cut_t], x_t, NT, preferred_element_type=F32)
            d_s = lax.dot_general(ws[half, :, cut_s], x_s, NT, preferred_element_type=F32)
            if ring.c == 0:
                raw_t[half] = d_t
                raw_s[half] = d_s
            else:
                raw_t[half] += d_t
                raw_s[half] += d_s

    r0.finish()
    multiply(r0)
    r2.column(2)
    r1.finish()
    multiply(r1)
    r2.finish()
    multiply(r2)
    r3.finish()
    multiply(r3)

    sums = [jnp.zeros((1, 128), F32) for _ in range(7)]
    for half in range(2):
        vocab0 = ((p * 2 + half) * RZ + z) * vloc
        ids = vocab0 + lax.broadcasted_iota(jnp.int32, (vloc, 128), 0)
        onehot = ids == labels
        rs = raw_s[half]
        tan_t = jnp.tanh(raw_t[half] * (1.0 / CAP))
        tan_s = jnp.tanh(rs * (1.0 / CAP))
        log_t = CAP * tan_t
        log_s = CAP * tan_s
        exp_t = jnp.exp(log_t)
        exp_s = jnp.exp(log_s)
        slope = 1.0 - tan_s * tan_s
        e_s = exp_s * slope
        e_t = exp_t * slope
        o_h = jnp.where(onehot, slope, 0.0)
        es_s[half] = e_s
        et_s[half] = e_t
        oh_s[half] = o_h
        terms = (
            exp_t, exp_s, exp_t * (log_t - log_s), jnp.where(onehot, log_s, 0.0),
            e_s * rs, e_t * rs, o_h * rs,
        )
        sums = [a + jnp.sum(v, axis=0, keepdims=True) for a, v in zip(sums, terms)]

    sxy[p] = jnp.concatenate(sums + [jnp.zeros((1, 128), F32)], axis=0)

    def a_copy(k):
        return remote(
            sxy.at[p], sxy.at[p], a_send.at[0], a_recv.at[0],
            at_plane((p + k) % PLANE),
        )

    def b_copy(k):
        return remote(
            sz.at[z], sz.at[z], b_send.at[0], b_recv.at[0],
            at_line((z + k) % RZ),
        )

    @pl.loop(1, PLANE)
    def _(k):
        a_copy(k).start()

    await_recv(sxy.at[pl.ds(0, PLANE - 1)], a_recv.at[0])

    sz[z] = jnp.sum(sxy[...], axis=0)

    @pl.loop(1, RZ)
    def _(k):
        b_copy(k).start()

    await_recv(sz.at[pl.ds(0, RZ - 1)], b_recv.at[0])

    total = jnp.sum(sz[...], axis=0)
    sum_t, sum_s, cross, picked = (total[i : i + 1] for i in range(4))
    scale_s = 2.0 / sum_s
    scale_t = 1.0 / sum_t

    for half in range(2):
        grad = es_s[half] * scale_s - et_s[half] * scale_t - oh_s[half]
        gbuf[:, half * vloc : (half + 1) * vloc] = grad.T.astype(BF16)
    part = 512
    for n in range(ds // part):
        cut = slice(n * part, (n + 1) * part)
        term = jnp.dot(
            gbuf[:, :vloc], ws[0, :, cut], preferred_element_type=F32
        ) + jnp.dot(gbuf[:, vloc:], ws[1, :, cut], preferred_element_type=F32)
        obuf[:, :, cut] = term.reshape(PLANE, 8, part).astype(BF16)

    def r_copy(k):
        to = (p + k) % PLANE
        return remote(
            obuf.at[to], rbuf.at[p], r_send.at[0], r_recv.at[0], at_plane(to)
        )

    @pl.loop(1, PLANE)
    def _(k):
        r_copy(k).start()

    loss = cross / sum_t - jnp.log(sum_t) + 2.0 * jnp.log(sum_s) - picked
    radial = scale_s * total[4:5] - scale_t * total[5:6] - total[6:7]
    packed = jnp.concatenate([loss, radial, jnp.zeros((6, 128), F32)], axis=0)
    cols[...] = packed.T
    mine = cols[pl.ds(p * 8, 8), :]
    out_ref[:, 256:] = pltpu.roll(packed, (128 - p * 8) % 128, 1)
    rad = mine[:, 1:2]

    rbuf[p] = obuf[p]

    await_recv(rbuf.at[pl.ds(0, PLANE - 1)], r_recv.at[0])

    back = jnp.sum(rbuf[...].astype(F32), axis=0) * gs[...]
    for k in range(RZ):
        zsend[k, :, :sl] = back[:, k * sl : (k + 1) * sl].astype(BF16)

    def q_copy(k):
        to = (z + k) % RZ
        return remote(
            zsend.at[to], zrecv.at[z], q_send.at[0], q_recv.at[0], at_line(to)
        )

    @pl.loop(1, RZ)
    def _(k):
        q_copy(k).start()

    await_send(buf.at[0, pl.ds(0, RZ - 1), 0], z_send.at[0])
    await_send(ibuf.at[pl.ds(0, PLANE - 1)], i_send.at[0])
    await_send(sxy.at[pl.ds(0, PLANE - 1)], a_send.at[0])
    await_send(sz.at[pl.ds(0, RZ - 1)], b_send.at[0])
    for ring in rings:
        await_send(buf.at[ring.q, pl.ds(0, 15)], g_send.at[ring.c])

    zrecv[z] = zsend[z]

    await_recv(zrecv.at[pl.ds(0, RZ - 1)], q_recv.at[0])

    sum_back = jnp.sum(zrecv[...].astype(F32), axis=0)[:, :sl]
    out = inv_s * sum_back - (inv_s * inv_s * rad) * sh_ref[...].astype(F32) / ds
    out_ref[:, :sl] = out

    await_send(obuf.at[pl.ds(0, PLANE - 1)], r_send.at[0])
    await_send(zsend.at[pl.ds(0, RZ - 1)], q_send.at[0])


def unpack(out_ref, loss_ref, grad_ref):
    loss_ref[...] = out_ref[0, 256 : 256 + loss_ref.shape[0]]
    grad_ref[...] = out_ref[:, : grad_ref.shape[1]].astype(BF16)


def on_device(th, sh, tg, sg, wt, ws, labels):
    tok, tl = th.shape
    sl = sh.shape[1]
    dt, ds, vloc = tl * RZ, sl * RZ, wt.shape[0]
    vmem = pl.BlockSpec(memory_space=pltpu.VMEM)
    hbm = pl.BlockSpec(memory_space=pl.ANY)
    dma = pltpu.SemaphoreType.DMA
    out = pl.pallas_call(
        kernel,
        out_shape=jax.ShapeDtypeStruct((tok, 384), F32),
        in_specs=[hbm] * 7,
        out_specs=vmem,
        scratch_shapes=[
            pltpu.VMEM((tok, tl), BF16),
            pltpu.VMEM((tok, sl), BF16),
            pltpu.VMEM((dt // 128, 128), BF16),
            pltpu.VMEM((ds // 128, 128), BF16),
            pltpu.VMEM((2, 128), jnp.int32),
            pltpu.VMEM((2, vloc, dt), BF16),
            pltpu.VMEM((2, vloc, ds), BF16),
            pltpu.VMEM((4, PLANE, 4, tok, tl + sl), BF16),
            pltpu.VMEM((PLANE, tok, 128), F32),
            pltpu.VMEM((1, dt), F32),
            pltpu.VMEM((1, ds), F32),
            pltpu.VMEM((2, vloc, 128), F32),
            pltpu.VMEM((2, vloc, 128), F32),
            pltpu.VMEM((2, vloc, 128), F32),
            pltpu.VMEM((2, vloc, 128), F32),
            pltpu.VMEM((2, vloc, 128), F32),
            pltpu.VMEM((PLANE, 8, 128), F32),
            pltpu.VMEM((RZ, 8, 128), F32),
            pltpu.VMEM((128, 2 * vloc), BF16),
            pltpu.VMEM((PLANE, tok, ds), BF16),
            pltpu.VMEM((PLANE, tok, ds), BF16),
            pltpu.VMEM((RZ, tok, 256), BF16),
            pltpu.VMEM((RZ, tok, 256), BF16),
            pltpu.VMEM((128, 8), F32),
            dma((2,)), dma((2,)), dma((2,)), dma((5,)),
            dma((1,)), dma((4,)),
            dma((4,)), dma((4, 8)),
            dma((1,)), dma((1,)),
            dma((1,)), dma((1,)),
            dma((1,)), dma((1,)),
            dma((1,)), dma((1,)),
            dma((1,)), dma((1,)),
        ],
        compiler_params=pltpu.CompilerParams(
            collective_id=0, has_side_effects=True, vmem_limit_bytes=56 * 1024 * 1024
        ),
    )(th, sh, tg.reshape(-1, 128), sg.reshape(-1, 128), labels.reshape(2, 128), wt, ws)
    return pl.pallas_call(
        unpack,
        out_shape=(
            jax.ShapeDtypeStruct((tok,), F32), jax.ShapeDtypeStruct((tok, sl), BF16)
        ),
        in_specs=[vmem],
        out_specs=(vmem, vmem),
    )(out)


def solution(mesh):
    in_specs = (
        P("dp", ("group", "tensor")),
        P("dp", ("group", "tensor")),
        P(),
        P(),
        P(("dp", "group", "tensor"), None),
        P(("dp", "group", "tensor"), None),
        P(),
    )
    out_specs = (P("dp"), P("dp", ("group", "tensor")))
    return jax.shard_map(
        on_device, mesh=mesh, in_specs=in_specs, out_specs=out_specs, check_vma=False
    )
```

```python
import jax
import jax.numpy as jnp
from jax import lax
from jax.experimental import pallas as pl
from jax.experimental.pallas import tpu as pltpu
from jax.sharding import PartitionSpec as P

CAP = 30.0
EPS = 1e-06
MESH = pl.DeviceIdType.MESH
F32 = jnp.float32
BF16 = jnp.bfloat16
RX, RY, RZ = 4, 4, 16
PLANE = RX * RY
NT = (((1,), (1,)), ((), ()))


def kernel(
    th_hbm, sh_hbm, tg_hbm, sg_hbm, lab_hbm, wt_hbm, ws_hbm,
    out_ref,
    th_ref, sh_ref, tg_ref, sg_ref, lab_ref, wt, ws, buf, ibuf, gt, gs, raw_t, raw_s, es_s, et_s, oh_s,
    sxy, sz, gbuf, obuf, rbuf, zsend, zrecv, cols,
    w_send, w_recv, w_loc, s_loc, z_send, z_recv, g_send, g_recv, i_send, i_recv,
    a_send, a_recv, b_send, b_recv, r_send, r_recv, q_send, q_recv,
):
    dp = lax.axis_index("dp")
    z = lax.axis_index("group") * 8 + lax.axis_index("tensor")
    core = dp % 2
    p = dp // 2
    x = p % RX
    y = p // RX
    quad = z // 4
    tl = th_ref.shape[1]
    sl = sh_ref.shape[1]
    ds = sl * RZ
    vloc = wt_hbm.shape[0]

    def at_plane(q):
        return (q * 2 + core, lax.axis_index("group"), lax.axis_index("tensor"))

    def at_line(k):
        return (dp, k // 8, k % 8)

    my_rows = pl.ds(pl.multiple_of(core * vloc, vloc), vloc)
    partner = (p * 2 + 1 - core, lax.axis_index("group"), lax.axis_index("tensor"))

    def remote(src, dst, send, recv, device):
        return pltpu.make_async_remote_copy(
            src_ref=src, dst_ref=dst, send_sem=send, recv_sem=recv,
            device_id=device, device_id_type=MESH,
        )

    small = [
        pltpu.make_async_copy(src, dst, s_loc.at[i])
        for i, (src, dst) in enumerate(
            (
                (th_hbm, th_ref), (sh_hbm, sh_ref), (tg_hbm, tg_ref),
                (sg_hbm, sg_ref), (lab_hbm, lab_ref),
            )
        )
    ]
    for copy in small:
        copy.start()

    barrier = pltpu.get_barrier_semaphore()

    @pl.loop(1, RZ)
    def _(k):
        pl.semaphore_signal(
            barrier, inc=1, device_id=at_line((z + k) % RZ), device_id_type=MESH
        )
        pl.semaphore_signal(
            barrier, inc=1, device_id=at_plane((p + k) % PLANE), device_id_type=MESH
        )

    pl.semaphore_signal(barrier, inc=1, device_id=partner, device_id_type=MESH)

    l_copies = [
        pltpu.make_async_copy(wt_hbm, wt.at[my_rows], w_loc.at[0]),
        pltpu.make_async_copy(ws_hbm, ws.at[my_rows], w_loc.at[1]),
    ]
    for copy in l_copies:
        copy.start()

    for copy in small:
        copy.wait()

    own = jnp.concatenate(
        [th_ref[...].astype(F32), sh_ref[...].astype(F32)], axis=1
    )
    buf[quad, p, z % 4] = own.astype(BF16)

    for gain_ref, wide in ((tg_ref, gt), (sg_ref, gs)):
        gain = gain_ref[...].astype(F32)
        for i in range(gain.shape[0]):
            wide[:, i * 128 : (i + 1) * 128] = gain[i : i + 1]

    lane = lax.broadcasted_iota(jnp.int32, (8, 128), 1)
    label_row = jnp.zeros((8, 128), jnp.int32)
    for q in range(PLANE):
        row = jnp.broadcast_to(lab_ref[q // 8 : q // 8 + 1, :], (8, 128))
        shift = (8 * q - 16 * (q % 8) - 8 * core + 256) % 128
        label_row = jnp.where(lane // 8 == q, pltpu.roll(row, shift, 1), label_row)
    labels = label_row[:1, :]

    pl.semaphore_wait(barrier, 31)

    def await_recv(ref, sem):
        remote(ref, ref, w_send.at[0], sem, partner).wait_recv()

    def await_send(ref, sem):
        remote(ref, ref, sem, w_recv.at[0], partner).wait_send()

    slab = buf.at[quad, p, z % 4]

    def z_start(k):
        to = (z + k + RZ) % RZ
        remote(
            slab, slab, z_send.at[0], z_recv.at[(quad - to // 4 + 4) % 4], at_line(to)
        ).start()

    @pl.loop(1, 8)
    def _(k):
        z_start(k)
        z_start(-k)

    z_start(8)

    w_copies = [
        remote(wt_hbm, wt.at[my_rows], w_send.at[0], w_recv.at[0], partner),
        remote(ws_hbm, ws.at[my_rows], w_send.at[1], w_recv.at[1], partner),
    ]
    for copy in w_copies:
        copy.start()

    class Ring:
        def __init__(self, c, delta, x_first, way):
            self.c, self.q, self.delta = c, (quad + delta) % 4, delta
            self.x_first, self.way = x_first, way
            self.me1, self.me2 = (x, y) if x_first else (y, x)
            self.alone = {
                ("first", 1): 0, ("first", -1): 1, ("far", 0): 2,
                ("second", 0): 3, ("second", -1): 4, ("second", 1): 5, ("second", 2): 6,
            }

        def src(self, o1, o2):
            i1, i2 = (self.me1 + o1 + 4) % 4, (self.me2 + o2 + 4) % 4
            return i2 * RX + i1 if self.x_first else i1 * RX + i2

        def send(self, o1, o2, to1, to2, sem):
            ref = buf.at[self.q, self.src(o1, o2)]
            remote(
                ref, ref, g_send.at[self.c], g_recv.at[self.c, sem],
                at_plane(self.src(to1, to2)),
            ).start()

        def wait(self, sem):
            await_recv(buf.at[self.q, p], g_recv.at[self.c, sem])

        def second(self, o):
            self.send(o, 0, 0, self.way, self.alone["second", o])
            self.send(o, 0, 0, -self.way, 7)

        def begin(self):
            n = 3 if self.c == 0 else 4
            await_recv(buf.at[self.q, p, pl.ds(0, n)], z_recv.at[self.delta])
            for to in (1, -1):
                self.send(0, 0, to, 0, self.alone["first", to])
            self.second(0)

        def near(self):
            way = self.way
            self.wait(self.alone["first", way])
            self.send(-way, 0, way, 0, self.alone["far", 0])
            self.second(-way)
            self.wait(self.alone["first", -way])
            self.second(way)

        def far(self):
            self.wait(self.alone["far", 0])
            self.second(2)

        def column(self, o):
            self.wait(self.alone["second", o])
            self.send(o, -self.way, 0, self.way, 7)

        def finish(self):
            await_recv(buf.at[self.q, pl.ds(0, 8)], g_recv.at[self.c, 7])

    class TwoStep(Ring):
        def begin(self):
            await_recv(buf.at[self.q, p], z_recv.at[self.delta])
            for sem, to in enumerate((1, -1, 2)):
                self.send(0, 0, to, 0, sem)
            for to in (1, -1, 2):
                self.send(0, 0, 0, to, 7)

        def middle(self):
            for sem, o in enumerate((-1, 1, 2)):
                self.wait(sem)
                for to in (1, -1, 2):
                    self.send(o, 0, 0, to, 7)

        def finish(self):
            await_recv(buf.at[self.q, pl.ds(0, 12)], g_recv.at[self.c, 7])


    class TwoStep(Ring):
        def begin(self):
            await_recv(buf.at[self.q, p], z_recv.at[self.delta])
            for sem, to in enumerate((1, -1, 2)):
                self.send(0, 0, to, 0, sem)
            for to in (1, -1, 2):
                self.send(0, 0, 0, to, 7)

        def middle(self):
            for sem, o in enumerate((-1, 1, 2)):
                self.wait(sem)
                for to in (1, -1, 2):
                    self.send(o, 0, 0, to, 7)

        def finish(self):
            await_recv(buf.at[self.q, pl.ds(0, 12)], g_recv.at[self.c, 7])

    beside = jnp.where(z % 4 < 2, 3, 1)
    r0, r1, r2, r3 = rings = [
        Ring(0, 0, True, 1), Ring(1, beside, False, 1),
        Ring(2, 4 - beside, True, -1), TwoStep(3, 2, False, -1),
    ]
    r0.begin()
    r1.begin()
    r0.near()
    r0.column(0)
    r2.begin()
    r3.begin()
    r1.near()
    r1.column(0)
    r0.far()
    r0.column(-1)
    r0.column(1)
    squares = jnp.zeros((8, tl + sl), F32)
    for k in range(4):
        for j in range(4):
            v = buf[k, p, j].astype(F32)
            squares = squares + v * v
    own_t = jnp.sum(squares[:, :tl], axis=1, keepdims=True)
    own_s = jnp.sum(squares[:, tl:], axis=1, keepdims=True)
    inv_t = lax.rsqrt(own_t / (tl * RZ) + EPS)
    inv_s = lax.rsqrt(own_s / ds + EPS)
    ibuf[p] = jnp.where(lane == 0, inv_t, inv_s)

    def i_copy(k):
        return remote(
            ibuf.at[p], ibuf.at[p], i_send.at[0], i_recv.at[0],
            at_plane((p + k) % PLANE),
        )

    @pl.loop(1, PLANE)
    def _(k):
        i_copy(k).start()

    r2.near()
    r2.column(0)
    r1.far()
    r1.column(-1)
    r1.column(1)
    r0.column(2)
    r3.middle()
    r2.far()
    r2.column(-1)
    r2.column(1)
    r1.column(2)
    await_recv(ibuf.at[pl.ds(0, PLANE - 1)], i_recv.at[0])
    for copy in l_copies:
        copy.wait()
    for copy in w_copies:
        copy.wait()

    all_t = ibuf[:, :, 0:1].reshape(PLANE * 8, 1)
    all_s = ibuf[:, :, 1:2].reshape(PLANE * 8, 1)

    def multiply(ring):
        pieces = [
            buf[ring.q, :, j].astype(F32).reshape(PLANE * 8, tl + sl) for j in range(4)
        ]
        cut_t = pl.ds(pl.multiple_of(ring.q * (4 * tl), 128), 4 * tl)
        cut_s = pl.ds(pl.multiple_of(ring.q * (4 * sl), 128), 4 * sl)
        v_t = jnp.concatenate([v[:, :tl] for v in pieces], axis=1)
        v_s = jnp.concatenate([v[:, tl:] for v in pieces], axis=1)
        x_t = (v_t * all_t * gt[:, cut_t]).astype(BF16)
        x_s = (v_s * all_s * gs[:, cut_s]).astype(BF16)
        d_t = lax.dot_general(wt[:, cut_t], x_t, NT, preferred_element_type=F32)
        d_s = lax.dot_general(ws[:, cut_s], x_s, NT, preferred_element_type=F32)
        if ring.c == 0:
            raw_t[...] = d_t
            raw_s[...] = d_s
        else:
            raw_t[...] += d_t
            raw_s[...] += d_s

    r0.finish()
    multiply(r0)
    r2.column(2)
    r1.finish()
    multiply(r1)
    r2.finish()
    multiply(r2)
    r3.finish()
    multiply(r3)

    sums = [jnp.zeros((1, 128), F32) for _ in range(7)]
    for half in range(2):
        vocab0 = ((p * 2 + half) * RZ + z) * vloc
        ids = vocab0 + lax.broadcasted_iota(jnp.int32, (vloc, 128), 0)
        onehot = ids == labels
        part = slice(half * vloc, (half + 1) * vloc)
        rs = raw_s[part]
        tan_t = jnp.tanh(raw_t[part] * (1.0 / CAP))
        tan_s = jnp.tanh(rs * (1.0 / CAP))
        log_t = CAP * tan_t
        log_s = CAP * tan_s
        exp_t = jnp.exp(log_t)
        exp_s = jnp.exp(log_s)
        slope = 1.0 - tan_s * tan_s
        e_s = exp_s * slope
        e_t = exp_t * slope
        o_h = jnp.where(onehot, slope, 0.0)
        es_s[half] = e_s
        et_s[half] = e_t
        oh_s[half] = o_h
        terms = (
            exp_t, exp_s, exp_t * (log_t - log_s), jnp.where(onehot, log_s, 0.0),
            e_s * rs, e_t * rs, o_h * rs,
        )
        sums = [a + jnp.sum(v, axis=0, keepdims=True) for a, v in zip(sums, terms)]

    sxy[p] = jnp.concatenate(sums + [jnp.zeros((1, 128), F32)], axis=0)

    def a_copy(k):
        return remote(
            sxy.at[p], sxy.at[p], a_send.at[0], a_recv.at[0],
            at_plane((p + k) % PLANE),
        )

    def b_copy(k):
        return remote(
            sz.at[z], sz.at[z], b_send.at[0], b_recv.at[0],
            at_line((z + k) % RZ),
        )

    @pl.loop(1, PLANE)
    def _(k):
        a_copy(k).start()

    await_recv(sxy.at[pl.ds(0, PLANE - 1)], a_recv.at[0])

    sz[z] = jnp.sum(sxy[...], axis=0)

    @pl.loop(1, RZ)
    def _(k):
        b_copy(k).start()

    await_recv(sz.at[pl.ds(0, RZ - 1)], b_recv.at[0])

    total = jnp.sum(sz[...], axis=0)
    sum_t, sum_s, cross, picked = (total[i : i + 1] for i in range(4))
    scale_s = 2.0 / sum_s
    scale_t = 1.0 / sum_t

    for half in range(2):
        grad = es_s[half] * scale_s - et_s[half] * scale_t - oh_s[half]
        gbuf[:, half * vloc : (half + 1) * vloc] = grad.T.astype(BF16)
    dh = ds // 2

    def r_copy(h, k):
        to = (p + k) % PLANE
        return remote(
            obuf.at[h, to], rbuf.at[h, p], r_send.at[h], r_recv.at[h], at_plane(to)
        )

    for h in range(2):
        part = dh // 2
        for n in range(2):
            lo = h * dh + n * part
            term = jnp.dot(gbuf[...], ws[:, lo : lo + part], preferred_element_type=F32)
            obuf[h, :, :, n * part : (n + 1) * part] = term.reshape(PLANE, 8, part).astype(BF16)

        @pl.loop(1, PLANE)
        def _(k):
            r_copy(h, k).start()

    loss = cross / sum_t - jnp.log(sum_t) + 2.0 * jnp.log(sum_s) - picked
    radial = scale_s * total[4:5] - scale_t * total[5:6] - total[6:7]
    packed = jnp.concatenate([loss, radial, jnp.zeros((6, 128), F32)], axis=0)
    cols[...] = packed.T
    mine = cols[pl.ds(p * 8, 8), :]
    out_ref[:, 256:] = pltpu.roll(packed, (128 - p * 8) % 128, 1)
    rad = mine[:, 1:2]

    for h in range(2):
        rbuf[h, p] = obuf[h, p]

    def q_start(h, k):
        to = h * 8 + (z + k) % 8

        @pl.when(to != z)
        def _():
            remote(
                zsend.at[to], zrecv.at[z], q_send.at[0], q_recv.at[0], at_line(to)
            ).start()

    for h in range(2):
        await_recv(rbuf.at[h, pl.ds(0, PLANE - 1)], r_recv.at[h])
        back = jnp.sum(rbuf[h].astype(F32), axis=0) * gs[:, h * dh : (h + 1) * dh]
        for k in range(8):
            zsend[h * 8 + k, :, :sl] = back[:, k * sl : (k + 1) * sl].astype(BF16)

        @pl.loop(0, 8)
        def _(k):
            q_start(h, k)

    await_send(buf.at[0, pl.ds(0, RZ - 1), 0], z_send.at[0])
    await_send(ibuf.at[pl.ds(0, PLANE - 1)], i_send.at[0])
    await_send(sxy.at[pl.ds(0, PLANE - 1)], a_send.at[0])
    await_send(sz.at[pl.ds(0, RZ - 1)], b_send.at[0])
    for ring in rings:
        await_send(buf.at[ring.q, pl.ds(0, 15)], g_send.at[ring.c])

    zrecv[z] = zsend[z]

    await_recv(zrecv.at[pl.ds(0, RZ - 1)], q_recv.at[0])

    sum_back = jnp.sum(zrecv[...].astype(F32), axis=0)[:, :sl]
    out = inv_s * sum_back - (inv_s * inv_s * rad) * sh_ref[...].astype(F32) / ds
    out_ref[:, :sl] = out

    for h in range(2):
        await_send(obuf.at[h, pl.ds(0, PLANE - 1)], r_send.at[h])
    await_send(zsend.at[pl.ds(0, RZ - 1)], q_send.at[0])


def unpack(out_ref, loss_ref, grad_ref):
    loss_ref[...] = out_ref[0, 256 : 256 + loss_ref.shape[0]]
    grad_ref[...] = out_ref[:, : grad_ref.shape[1]].astype(BF16)


def on_device(th, sh, tg, sg, wt, ws, labels):
    tok, tl = th.shape
    sl = sh.shape[1]
    dt, ds, vloc = tl * RZ, sl * RZ, wt.shape[0]
    vmem = pl.BlockSpec(memory_space=pltpu.VMEM)
    hbm = pl.BlockSpec(memory_space=pl.ANY)
    dma = pltpu.SemaphoreType.DMA
    out = pl.pallas_call(
        kernel,
        out_shape=jax.ShapeDtypeStruct((tok, 384), F32),
        in_specs=[hbm] * 7,
        out_specs=vmem,
        scratch_shapes=[
            pltpu.VMEM((tok, tl), BF16),
            pltpu.VMEM((tok, sl), BF16),
            pltpu.VMEM((dt // 128, 128), BF16),
            pltpu.VMEM((ds // 128, 128), BF16),
            pltpu.VMEM((2, 128), jnp.int32),
            pltpu.VMEM((2 * vloc, dt), BF16),
            pltpu.VMEM((2 * vloc, ds), BF16),
            pltpu.VMEM((4, PLANE, 4, tok, tl + sl), BF16),
            pltpu.VMEM((PLANE, tok, 128), F32),
            pltpu.VMEM((1, dt), F32),
            pltpu.VMEM((1, ds), F32),
            pltpu.VMEM((2 * vloc, 128), F32),
            pltpu.VMEM((2 * vloc, 128), F32),
            pltpu.VMEM((2, vloc, 128), F32),
            pltpu.VMEM((2, vloc, 128), F32),
            pltpu.VMEM((2, vloc, 128), F32),
            pltpu.VMEM((PLANE, 8, 128), F32),
            pltpu.VMEM((RZ, 8, 128), F32),
            pltpu.VMEM((128, 2 * vloc), BF16),
            pltpu.VMEM((2, PLANE, tok, ds // 2), BF16),
            pltpu.VMEM((2, PLANE, tok, ds // 2), BF16),
            pltpu.VMEM((RZ, tok, 256), BF16),
            pltpu.VMEM((RZ, tok, 256), BF16),
            pltpu.VMEM((128, 8), F32),
            dma((2,)), dma((2,)), dma((2,)), dma((5,)),
            dma((1,)), dma((4,)),
            dma((4,)), dma((4, 8)),
            dma((1,)), dma((1,)),
            dma((1,)), dma((1,)),
            dma((1,)), dma((1,)),
            dma((2,)), dma((2,)),
            dma((1,)), dma((1,)),
        ],
        compiler_params=pltpu.CompilerParams(
            collective_id=0, has_side_effects=True, vmem_limit_bytes=56 * 1024 * 1024
        ),
    )(th, sh, tg.reshape(-1, 128), sg.reshape(-1, 128), labels.reshape(2, 128), wt, ws)
    return pl.pallas_call(
        unpack,
        out_shape=(
            jax.ShapeDtypeStruct((tok,), F32), jax.ShapeDtypeStruct((tok, sl), BF16)
        ),
        in_specs=[vmem],
        out_specs=(vmem, vmem),
    )(out)


def solution(mesh):
    in_specs = (
        P("dp", ("group", "tensor")),
        P("dp", ("group", "tensor")),
        P(),
        P(),
        P(("dp", "group", "tensor"), None),
        P(("dp", "group", "tensor"), None),
        P(),
    )
    out_specs = (P("dp"), P("dp", ("group", "tensor")))
    return jax.shard_map(
        on_device, mesh=mesh, in_specs=in_specs, out_specs=out_specs, check_vma=False
    )
```

```python
import jax
import jax.numpy as jnp
from jax import lax
from jax.experimental import pallas as pl
from jax.experimental.pallas import tpu as pltpu
from jax.sharding import PartitionSpec as P

CAP = 30.0
EPS = 1e-06
MESH = pl.DeviceIdType.MESH
F32 = jnp.float32
BF16 = jnp.bfloat16
PARTS = 4
RX, RY, RZ = 4, 4, 16
PLANE = RX * RY
NT = (((1,), (1,)), ((), ()))


def kernel(
    th_hbm, sh_hbm, tg_hbm, sg_hbm, lab_hbm, wt_hbm, ws_hbm,
    out_ref,
    th_ref, sh_ref, tg_ref, sg_ref, lab_ref, wt, ws, buf, ibuf, gt, gs, raw_t, raw_s, es_s, et_s, oh_s,
    sxy, sz, gbuf, obuf, rbuf, zsend, zrecv, cols,
    w_send, w_recv, w_loc, s_loc, z_send, z_recv, g_send, g_recv, i_send, i_recv,
    a_send, a_recv, b_send, b_recv, r_send, r_recv, q_send, q_recv,
):
    dp = lax.axis_index("dp")
    z = lax.axis_index("group") * 8 + lax.axis_index("tensor")
    core = dp % 2
    p = dp // 2
    x = p % RX
    y = p // RX
    quad = z // 4
    tl = th_ref.shape[1]
    sl = sh_ref.shape[1]
    ds = sl * RZ
    vloc = wt_hbm.shape[0]

    def at_plane(q):
        return (q * 2 + core, lax.axis_index("group"), lax.axis_index("tensor"))

    def at_line(k):
        return (dp, k // 8, k % 8)

    my_rows = pl.ds(pl.multiple_of(core * vloc, vloc), vloc)
    partner = (p * 2 + 1 - core, lax.axis_index("group"), lax.axis_index("tensor"))

    def remote(src, dst, send, recv, device):
        return pltpu.make_async_remote_copy(
            src_ref=src, dst_ref=dst, send_sem=send, recv_sem=recv,
            device_id=device, device_id_type=MESH,
        )

    small = [
        pltpu.make_async_copy(src, dst, s_loc.at[i])
        for i, (src, dst) in enumerate(
            (
                (th_hbm, th_ref), (sh_hbm, sh_ref), (tg_hbm, tg_ref),
                (sg_hbm, sg_ref), (lab_hbm, lab_ref),
            )
        )
    ]
    for copy in small:
        copy.start()

    barrier = pltpu.get_barrier_semaphore()

    @pl.loop(1, RZ)
    def _(k):
        pl.semaphore_signal(
            barrier, inc=1, device_id=at_line((z + k) % RZ), device_id_type=MESH
        )
        pl.semaphore_signal(
            barrier, inc=1, device_id=at_plane((p + k) % PLANE), device_id_type=MESH
        )

    pl.semaphore_signal(barrier, inc=1, device_id=partner, device_id_type=MESH)

    l_copies = [
        pltpu.make_async_copy(wt_hbm, wt.at[my_rows], w_loc.at[0]),
        pltpu.make_async_copy(ws_hbm, ws.at[my_rows], w_loc.at[1]),
    ]
    for copy in l_copies:
        copy.start()

    for copy in small:
        copy.wait()

    own = jnp.concatenate(
        [th_ref[...].astype(F32), sh_ref[...].astype(F32)], axis=1
    )
    buf[quad, p, z % 4] = own.astype(BF16)

    for gain_ref, wide in ((tg_ref, gt), (sg_ref, gs)):
        gain = gain_ref[...].astype(F32)
        for i in range(gain.shape[0]):
            wide[:, i * 128 : (i + 1) * 128] = gain[i : i + 1]

    lane = lax.broadcasted_iota(jnp.int32, (8, 128), 1)
    label_row = jnp.zeros((8, 128), jnp.int32)
    for q in range(PLANE):
        row = jnp.broadcast_to(lab_ref[q // 8 : q // 8 + 1, :], (8, 128))
        shift = (8 * q - 16 * (q % 8) - 8 * core + 256) % 128
        label_row = jnp.where(lane // 8 == q, pltpu.roll(row, shift, 1), label_row)
    labels = label_row[:1, :]

    pl.semaphore_wait(barrier, 31)

    def await_recv(ref, sem):
        remote(ref, ref, w_send.at[0], sem, partner).wait_recv()

    def await_send(ref, sem):
        remote(ref, ref, sem, w_recv.at[0], partner).wait_send()

    slab = buf.at[quad, p, z % 4]

    def z_start(k):
        to = (z + k + RZ) % RZ
        remote(
            slab, slab, z_send.at[0], z_recv.at[(quad - to // 4 + 4) % 4], at_line(to)
        ).start()

    @pl.loop(1, 8)
    def _(k):
        z_start(k)
        z_start(-k)

    z_start(8)

    w_copies = [
        remote(wt_hbm, wt.at[my_rows], w_send.at[0], w_recv.at[0], partner),
        remote(ws_hbm, ws.at[my_rows], w_send.at[1], w_recv.at[1], partner),
    ]
    for copy in w_copies:
        copy.start()

    class Ring:
        def __init__(self, c, delta, x_first, way):
            self.c, self.q, self.delta = c, (quad + delta) % 4, delta
            self.x_first, self.way = x_first, way
            self.me1, self.me2 = (x, y) if x_first else (y, x)
            self.alone = {
                ("first", 1): 0, ("first", -1): 1, ("far", 0): 2,
                ("second", 0): 3, ("second", -1): 4, ("second", 1): 5, ("second", 2): 6,
            }

        def src(self, o1, o2):
            i1, i2 = (self.me1 + o1 + 4) % 4, (self.me2 + o2 + 4) % 4
            return i2 * RX + i1 if self.x_first else i1 * RX + i2

        def send(self, o1, o2, to1, to2, sem):
            ref = buf.at[self.q, self.src(o1, o2)]
            remote(
                ref, ref, g_send.at[self.c], g_recv.at[self.c, sem],
                at_plane(self.src(to1, to2)),
            ).start()

        def wait(self, sem):
            await_recv(buf.at[self.q, p], g_recv.at[self.c, sem])

        def second(self, o):
            self.send(o, 0, 0, self.way, self.alone["second", o])
            self.send(o, 0, 0, -self.way, 7)

        def begin(self):
            n = 3 if self.c == 0 else 4
            await_recv(buf.at[self.q, p, pl.ds(0, n)], z_recv.at[self.delta])
            for to in (1, -1):
                self.send(0, 0, to, 0, self.alone["first", to])
            self.second(0)

        def near(self):
            way = self.way
            self.wait(self.alone["first", way])
            self.send(-way, 0, way, 0, self.alone["far", 0])
            self.second(-way)
            self.wait(self.alone["first", -way])
            self.second(way)

        def far(self):
            self.wait(self.alone["far", 0])
            self.second(2)

        def column(self, o):
            self.wait(self.alone["second", o])
            self.send(o, -self.way, 0, self.way, 7)

        def finish(self):
            await_recv(buf.at[self.q, pl.ds(0, 8)], g_recv.at[self.c, 7])

    class TwoStep(Ring):
        def begin(self):
            await_recv(buf.at[self.q, p], z_recv.at[self.delta])
            for sem, to in enumerate((1, -1, 2)):
                self.send(0, 0, to, 0, sem)
            for to in (1, -1, 2):
                self.send(0, 0, 0, to, 7)

        def middle(self):
            for sem, o in enumerate((-1, 1, 2)):
                self.wait(sem)
                for to in (1, -1, 2):
                    self.send(o, 0, 0, to, 7)

        def finish(self):
            await_recv(buf.at[self.q, pl.ds(0, 12)], g_recv.at[self.c, 7])


    class TwoStep(Ring):
        def begin(self):
            await_recv(buf.at[self.q, p], z_recv.at[self.delta])
            for sem, to in enumerate((1, -1, 2)):
                self.send(0, 0, to, 0, sem)
            for to in (1, -1, 2):
                self.send(0, 0, 0, to, 7)

        def middle(self):
            for sem, o in enumerate((-1, 1, 2)):
                self.wait(sem)
                for to in (1, -1, 2):
                    self.send(o, 0, 0, to, 7)

        def finish(self):
            await_recv(buf.at[self.q, pl.ds(0, 12)], g_recv.at[self.c, 7])

    beside = jnp.where(z % 4 < 2, 3, 1)
    r0, r1, r2, r3 = rings = [
        Ring(0, 0, True, 1), Ring(1, beside, False, 1),
        Ring(2, 4 - beside, True, -1), TwoStep(3, 2, False, -1),
    ]
    r0.begin()
    r1.begin()
    r0.near()
    r0.column(0)
    r2.begin()
    r3.begin()
    r1.near()
    r1.column(0)
    r0.far()
    r0.column(-1)
    r0.column(1)
    squares = jnp.zeros((8, tl + sl), F32)
    for k in range(4):
        for j in range(4):
            v = buf[k, p, j].astype(F32)
            squares = squares + v * v
    own_t = jnp.sum(squares[:, :tl], axis=1, keepdims=True)
    own_s = jnp.sum(squares[:, tl:], axis=1, keepdims=True)
    inv_t = lax.rsqrt(own_t / (tl * RZ) + EPS)
    inv_s = lax.rsqrt(own_s / ds + EPS)
    ibuf[p] = jnp.where(lane == 0, inv_t, inv_s)

    def i_copy(k):
        return remote(
            ibuf.at[p], ibuf.at[p], i_send.at[0], i_recv.at[0],
            at_plane((p + k) % PLANE),
        )

    @pl.loop(1, PLANE)
    def _(k):
        i_copy(k).start()

    r2.near()
    r2.column(0)
    r1.far()
    r1.column(-1)
    r1.column(1)
    r0.column(2)
    r3.middle()
    r2.far()
    r2.column(-1)
    r2.column(1)
    r1.column(2)
    await_recv(ibuf.at[pl.ds(0, PLANE - 1)], i_recv.at[0])
    for copy in l_copies:
        copy.wait()
    for copy in w_copies:
        copy.wait()

    all_t = ibuf[:, :, 0:1].reshape(PLANE * 8, 1)
    all_s = ibuf[:, :, 1:2].reshape(PLANE * 8, 1)

    def multiply(ring):
        pieces = [
            buf[ring.q, :, j].astype(F32).reshape(PLANE * 8, tl + sl) for j in range(4)
        ]
        cut_t = pl.ds(pl.multiple_of(ring.q * (4 * tl), 128), 4 * tl)
        cut_s = pl.ds(pl.multiple_of(ring.q * (4 * sl), 128), 4 * sl)
        v_t = jnp.concatenate([v[:, :tl] for v in pieces], axis=1)
        v_s = jnp.concatenate([v[:, tl:] for v in pieces], axis=1)
        x_t = (v_t * all_t * gt[:, cut_t]).astype(BF16)
        x_s = (v_s * all_s * gs[:, cut_s]).astype(BF16)
        d_t = lax.dot_general(wt[:, cut_t], x_t, NT, preferred_element_type=F32)
        d_s = lax.dot_general(ws[:, cut_s], x_s, NT, preferred_element_type=F32)
        if ring.c == 0:
            raw_t[...] = d_t
            raw_s[...] = d_s
        else:
            raw_t[...] += d_t
            raw_s[...] += d_s

    r0.finish()
    multiply(r0)
    r2.column(2)
    r1.finish()
    multiply(r1)
    r2.finish()
    r3.finish()
    multiply(r2)
    multiply(r3)

    sums = [jnp.zeros((1, 128), F32) for _ in range(7)]
    for half in range(2):
        vocab0 = ((p * 2 + half) * RZ + z) * vloc
        ids = vocab0 + lax.broadcasted_iota(jnp.int32, (vloc, 128), 0)
        onehot = ids == labels
        part = slice(half * vloc, (half + 1) * vloc)
        rs = raw_s[part]
        tan_t = jnp.tanh(raw_t[part] * (1.0 / CAP))
        tan_s = jnp.tanh(rs * (1.0 / CAP))
        log_t = CAP * tan_t
        log_s = CAP * tan_s
        exp_t = jnp.exp(log_t)
        exp_s = jnp.exp(log_s)
        slope = 1.0 - tan_s * tan_s
        e_s = exp_s * slope
        e_t = exp_t * slope
        o_h = jnp.where(onehot, slope, 0.0)
        es_s[half] = e_s
        et_s[half] = e_t
        oh_s[half] = o_h
        terms = (
            exp_t, exp_s, exp_t * (log_t - log_s), jnp.where(onehot, log_s, 0.0),
            e_s * rs, e_t * rs, o_h * rs,
        )
        sums = [a + jnp.sum(v, axis=0, keepdims=True) for a, v in zip(sums, terms)]

    sxy[p] = jnp.concatenate(sums + [jnp.zeros((1, 128), F32)], axis=0)

    def a_copy(k):
        return remote(
            sxy.at[p], sxy.at[p], a_send.at[0], a_recv.at[0],
            at_plane((p + k) % PLANE),
        )

    def b_copy(k):
        return remote(
            sz.at[z], sz.at[z], b_send.at[0], b_recv.at[0],
            at_line((z + k) % RZ),
        )

    @pl.loop(1, PLANE)
    def _(k):
        a_copy(k).start()

    await_recv(sxy.at[pl.ds(0, PLANE - 1)], a_recv.at[0])

    sz[z] = jnp.sum(sxy[...], axis=0)

    @pl.loop(1, RZ)
    def _(k):
        b_copy(k).start()

    await_recv(sz.at[pl.ds(0, RZ - 1)], b_recv.at[0])

    total = jnp.sum(sz[...], axis=0)
    sum_t, sum_s, cross, picked = (total[i : i + 1] for i in range(4))
    scale_s = 2.0 / sum_s
    scale_t = 1.0 / sum_t

    for half in range(2):
        grad = es_s[half] * scale_s - et_s[half] * scale_t - oh_s[half]
        gbuf[:, half * vloc : (half + 1) * vloc] = grad.T.astype(BF16)
    dh = ds // PARTS

    def r_copy(h, k):
        to = (p + k) % PLANE
        return remote(
            obuf.at[h, to], rbuf.at[h, p], r_send.at[h], r_recv.at[h], at_plane(to)
        )

    for h in range(PARTS):
        term = jnp.dot(
            gbuf[...], ws[:, h * dh : (h + 1) * dh], preferred_element_type=F32
        )
        obuf[h] = term.reshape(PLANE, 8, dh).astype(BF16)

        @pl.loop(1, PLANE)
        def _(k):
            r_copy(h, k).start()

    loss = cross / sum_t - jnp.log(sum_t) + 2.0 * jnp.log(sum_s) - picked
    radial = scale_s * total[4:5] - scale_t * total[5:6] - total[6:7]
    packed = jnp.concatenate([loss, radial, jnp.zeros((6, 128), F32)], axis=0)
    cols[...] = packed.T
    mine = cols[pl.ds(p * 8, 8), :]
    out_ref[:, 256:] = pltpu.roll(packed, (128 - p * 8) % 128, 1)
    rad = mine[:, 1:2]

    for h in range(PARTS):
        rbuf[h, p] = obuf[h, p]

    def q_start(h, k):
        to = h * (RZ // PARTS) + (z + k) % (RZ // PARTS)

        @pl.when(to != z)
        def _():
            remote(
                zsend.at[to], zrecv.at[z], q_send.at[0], q_recv.at[0], at_line(to)
            ).start()

    for h in range(PARTS):
        await_recv(rbuf.at[h, pl.ds(0, PLANE - 1)], r_recv.at[h])
        back = jnp.sum(rbuf[h].astype(F32), axis=0) * gs[:, h * dh : (h + 1) * dh]
        for k in range(RZ // PARTS):
            zsend[h * (RZ // PARTS) + k, :, :sl] = back[:, k * sl : (k + 1) * sl].astype(BF16)

        @pl.loop(0, RZ // PARTS)
        def _(k):
            q_start(h, k)

    await_send(buf.at[0, pl.ds(0, RZ - 1), 0], z_send.at[0])
    await_send(ibuf.at[pl.ds(0, PLANE - 1)], i_send.at[0])
    await_send(sxy.at[pl.ds(0, PLANE - 1)], a_send.at[0])
    await_send(sz.at[pl.ds(0, RZ - 1)], b_send.at[0])
    for ring in rings:
        await_send(buf.at[ring.q, pl.ds(0, 15)], g_send.at[ring.c])

    zrecv[z] = zsend[z]

    await_recv(zrecv.at[pl.ds(0, RZ - 1)], q_recv.at[0])

    sum_back = jnp.sum(zrecv[...].astype(F32), axis=0)[:, :sl]
    out = inv_s * sum_back - (inv_s * inv_s * rad) * sh_ref[...].astype(F32) / ds
    out_ref[:, :sl] = out

    for h in range(PARTS):
        await_send(obuf.at[h, pl.ds(0, PLANE - 1)], r_send.at[h])
    await_send(zsend.at[pl.ds(0, RZ - 1)], q_send.at[0])


def unpack(out_ref, loss_ref, grad_ref):
    loss_ref[...] = out_ref[0, 256 : 256 + loss_ref.shape[0]]
    grad_ref[...] = out_ref[:, : grad_ref.shape[1]].astype(BF16)


def on_device(th, sh, tg, sg, wt, ws, labels):
    tok, tl = th.shape
    sl = sh.shape[1]
    dt, ds, vloc = tl * RZ, sl * RZ, wt.shape[0]
    vmem = pl.BlockSpec(memory_space=pltpu.VMEM)
    hbm = pl.BlockSpec(memory_space=pl.ANY)
    dma = pltpu.SemaphoreType.DMA
    out = pl.pallas_call(
        kernel,
        out_shape=jax.ShapeDtypeStruct((tok, 384), F32),
        in_specs=[hbm] * 7,
        out_specs=vmem,
        scratch_shapes=[
            pltpu.VMEM((tok, tl), BF16),
            pltpu.VMEM((tok, sl), BF16),
            pltpu.VMEM((dt // 128, 128), BF16),
            pltpu.VMEM((ds // 128, 128), BF16),
            pltpu.VMEM((2, 128), jnp.int32),
            pltpu.VMEM((2 * vloc, dt), BF16),
            pltpu.VMEM((2 * vloc, ds), BF16),
            pltpu.VMEM((4, PLANE, 4, tok, tl + sl), BF16),
            pltpu.VMEM((PLANE, tok, 128), F32),
            pltpu.VMEM((1, dt), F32),
            pltpu.VMEM((1, ds), F32),
            pltpu.VMEM((2 * vloc, 128), F32),
            pltpu.VMEM((2 * vloc, 128), F32),
            pltpu.VMEM((2, vloc, 128), F32),
            pltpu.VMEM((2, vloc, 128), F32),
            pltpu.VMEM((2, vloc, 128), F32),
            pltpu.VMEM((PLANE, 8, 128), F32),
            pltpu.VMEM((RZ, 8, 128), F32),
            pltpu.VMEM((128, 2 * vloc), BF16),
            pltpu.VMEM((PARTS, PLANE, tok, ds // PARTS), BF16),
            pltpu.VMEM((PARTS, PLANE, tok, ds // PARTS), BF16),
            pltpu.VMEM((RZ, tok, 256), BF16),
            pltpu.VMEM((RZ, tok, 256), BF16),
            pltpu.VMEM((128, 8), F32),
            dma((2,)), dma((2,)), dma((2,)), dma((5,)),
            dma((1,)), dma((4,)),
            dma((4,)), dma((4, 8)),
            dma((1,)), dma((1,)),
            dma((1,)), dma((1,)),
            dma((1,)), dma((1,)),
            dma((PARTS,)), dma((PARTS,)),
            dma((1,)), dma((1,)),
        ],
        compiler_params=pltpu.CompilerParams(
            collective_id=0, has_side_effects=True, vmem_limit_bytes=56 * 1024 * 1024
        ),
    )(th, sh, tg.reshape(-1, 128), sg.reshape(-1, 128), labels.reshape(2, 128), wt, ws)
    return pl.pallas_call(
        unpack,
        out_shape=(
            jax.ShapeDtypeStruct((tok,), F32), jax.ShapeDtypeStruct((tok, sl), BF16)
        ),
        in_specs=[vmem],
        out_specs=(vmem, vmem),
    )(out)


def solution(mesh):
    in_specs = (
        P("dp", ("group", "tensor")),
        P("dp", ("group", "tensor")),
        P(),
        P(),
        P(("dp", "group", "tensor"), None),
        P(("dp", "group", "tensor"), None),
        P(),
    )
    out_specs = (P("dp"), P("dp", ("group", "tensor")))
    return jax.shard_map(
        on_device, mesh=mesh, in_specs=in_specs, out_specs=out_specs, check_vma=False
    )
```

```python
import jax
import jax.numpy as jnp
from jax import lax
from jax.experimental import pallas as pl
from jax.experimental.pallas import tpu as pltpu
from jax.sharding import PartitionSpec as P

CAP = 30.0
EPS = 1e-06
MESH = pl.DeviceIdType.MESH
F32 = jnp.float32
BF16 = jnp.bfloat16
PARTS = 4
RX, RY, RZ = 4, 4, 16
PLANE = RX * RY
NT = (((1,), (1,)), ((), ()))


def kernel(
    th_hbm, sh_hbm, tg_hbm, sg_hbm, lab_hbm, wt_hbm, ws_hbm,
    out_ref,
    th_ref, sh_ref, tg_ref, sg_ref, lab_ref, wt, ws, buf, ibuf, gt, gs, raw_t, raw_s, es_s, et_s, oh_s,
    sxy, sz, gbuf, obuf, rbuf, zsend, zrecv, cols,
    w_send, w_recv, w_loc, s_loc, z_send, z_recv, g_send, g_recv, i_send, i_recv,
    a_send, a_recv, b_send, b_recv, r_send, r_recv, q_send, q_recv,
):
    dp = lax.axis_index("dp")
    z = lax.axis_index("group") * 8 + lax.axis_index("tensor")
    core = dp % 2
    p = dp // 2
    x = p % RX
    y = p // RX
    quad = z // 4
    tl = th_ref.shape[1]
    sl = sh_ref.shape[1]
    ds = sl * RZ
    vloc = wt_hbm.shape[0]

    def at_plane(q):
        return (q * 2 + core, lax.axis_index("group"), lax.axis_index("tensor"))

    def at_line(k):
        return (dp, k // 8, k % 8)

    my_rows = pl.ds(pl.multiple_of(core * vloc, vloc), vloc)
    partner = (p * 2 + 1 - core, lax.axis_index("group"), lax.axis_index("tensor"))

    def remote(src, dst, send, recv, device):
        return pltpu.make_async_remote_copy(
            src_ref=src, dst_ref=dst, send_sem=send, recv_sem=recv,
            device_id=device, device_id_type=MESH,
        )

    small = [
        pltpu.make_async_copy(src, dst, s_loc.at[i])
        for i, (src, dst) in enumerate(
            (
                (th_hbm, th_ref), (sh_hbm, sh_ref), (tg_hbm, tg_ref),
                (sg_hbm, sg_ref), (lab_hbm, lab_ref),
            )
        )
    ]
    for copy in small:
        copy.start()

    barrier = pltpu.get_barrier_semaphore()

    @pl.loop(1, RZ)
    def _(k):
        pl.semaphore_signal(
            barrier, inc=1, device_id=at_line((z + k) % RZ), device_id_type=MESH
        )
        pl.semaphore_signal(
            barrier, inc=1, device_id=at_plane((p + k) % PLANE), device_id_type=MESH
        )

    pl.semaphore_signal(barrier, inc=1, device_id=partner, device_id_type=MESH)

    l_copies = [
        pltpu.make_async_copy(wt_hbm, wt.at[my_rows], w_loc.at[0]),
        pltpu.make_async_copy(ws_hbm, ws.at[my_rows], w_loc.at[1]),
    ]
    for copy in l_copies:
        copy.start()

    for copy in small:
        copy.wait()

    own = jnp.concatenate(
        [th_ref[...].astype(F32), sh_ref[...].astype(F32)], axis=1
    )
    buf[quad, p, z % 4] = own.astype(BF16)

    for gain_ref, wide in ((tg_ref, gt), (sg_ref, gs)):
        gain = gain_ref[...].astype(F32)
        for i in range(gain.shape[0]):
            wide[:, i * 128 : (i + 1) * 128] = gain[i : i + 1]

    lane = lax.broadcasted_iota(jnp.int32, (8, 128), 1)
    label_row = jnp.zeros((8, 128), jnp.int32)
    for q in range(PLANE):
        row = jnp.broadcast_to(lab_ref[q // 8 : q // 8 + 1, :], (8, 128))
        shift = (8 * q - 16 * (q % 8) - 8 * core + 256) % 128
        label_row = jnp.where(lane // 8 == q, pltpu.roll(row, shift, 1), label_row)
    labels = label_row[:1, :]

    pl.semaphore_wait(barrier, 31)

    def await_recv(ref, sem):
        remote(ref, ref, w_send.at[0], sem, partner).wait_recv()

    def await_send(ref, sem):
        remote(ref, ref, sem, w_recv.at[0], partner).wait_send()

    slab = buf.at[quad, p, z % 4]

    def z_start(k):
        to = (z + k + RZ) % RZ
        remote(
            slab, slab, z_send.at[0], z_recv.at[(quad - to // 4 + 4) % 4], at_line(to)
        ).start()

    @pl.loop(1, 8)
    def _(k):
        z_start(k)
        z_start(-k)

    z_start(8)

    w_copies = [
        remote(wt_hbm, wt.at[my_rows], w_send.at[0], w_recv.at[0], partner),
        remote(ws_hbm, ws.at[my_rows], w_send.at[1], w_recv.at[1], partner),
    ]
    for copy in w_copies:
        copy.start()

    class Ring:
        def __init__(self, c, delta, x_first, way):
            self.c, self.q, self.delta = c, (quad + delta) % 4, delta
            self.x_first, self.way = x_first, way
            self.me1, self.me2 = (x, y) if x_first else (y, x)
            self.alone = {
                ("first", 1): 0, ("first", -1): 1, ("far", 0): 2,
                ("second", 0): 3, ("second", -1): 4, ("second", 1): 5, ("second", 2): 6,
            }

        def src(self, o1, o2):
            i1, i2 = (self.me1 + o1 + 4) % 4, (self.me2 + o2 + 4) % 4
            return i2 * RX + i1 if self.x_first else i1 * RX + i2

        def send(self, o1, o2, to1, to2, sem):
            ref = buf.at[self.q, self.src(o1, o2)]
            remote(
                ref, ref, g_send.at[self.c], g_recv.at[self.c, sem],
                at_plane(self.src(to1, to2)),
            ).start()

        def wait(self, sem):
            await_recv(buf.at[self.q, p], g_recv.at[self.c, sem])

        def second(self, o):
            self.send(o, 0, 0, self.way, self.alone["second", o])
            self.send(o, 0, 0, -self.way, 7)

        def begin(self):
            n = 3 if self.c == 0 else 4
            await_recv(buf.at[self.q, p, pl.ds(0, n)], z_recv.at[self.delta])
            for to in (1, -1):
                self.send(0, 0, to, 0, self.alone["first", to])
            self.second(0)

        def near(self):
            way = self.way
            self.wait(self.alone["first", way])
            self.send(-way, 0, way, 0, self.alone["far", 0])
            self.second(-way)
            self.wait(self.alone["first", -way])
            self.second(way)

        def far(self):
            self.wait(self.alone["far", 0])
            self.second(2)

        def column(self, o):
            self.wait(self.alone["second", o])
            self.send(o, -self.way, 0, self.way, 7)

        def finish(self):
            await_recv(buf.at[self.q, pl.ds(0, 8)], g_recv.at[self.c, 7])

    class TwoStep(Ring):
        def begin(self):
            await_recv(buf.at[self.q, p], z_recv.at[self.delta])
            for sem, to in enumerate((1, -1, 2)):
                self.send(0, 0, to, 0, sem)
            for to in (1, -1, 2):
                self.send(0, 0, 0, to, 7)

        def middle(self):
            for sem, o in enumerate((-1, 1, 2)):
                self.wait(sem)
                for to in (1, -1, 2):
                    self.send(o, 0, 0, to, 7)

        def finish(self):
            await_recv(buf.at[self.q, pl.ds(0, 12)], g_recv.at[self.c, 7])


    class TwoStep(Ring):
        def begin(self):
            await_recv(buf.at[self.q, p], z_recv.at[self.delta])
            for sem, to in enumerate((1, -1, 2)):
                self.send(0, 0, to, 0, sem)
            for to in (1, -1, 2):
                self.send(0, 0, 0, to, 7)

        def middle(self):
            for sem, o in enumerate((-1, 1, 2)):
                self.wait(sem)
                for to in (1, -1, 2):
                    self.send(o, 0, 0, to, 7)

        def finish(self):
            await_recv(buf.at[self.q, pl.ds(0, 12)], g_recv.at[self.c, 7])

    beside = jnp.where(z % 4 < 2, 3, 1)
    r0, r1, r2, r3 = rings = [
        Ring(0, 0, True, 1), Ring(1, beside, False, 1),
        Ring(2, 4 - beside, True, -1), TwoStep(3, 2, False, -1),
    ]
    r0.begin()
    r1.begin()
    r0.near()
    r0.column(0)
    r2.begin()
    r3.begin()
    r1.near()
    r1.column(0)
    r0.far()
    r0.column(-1)
    r0.column(1)
    squares = jnp.zeros((8, tl + sl), F32)
    for k in range(4):
        for j in range(4):
            v = buf[k, p, j].astype(F32)
            squares = squares + v * v
    own_t = jnp.sum(squares[:, :tl], axis=1, keepdims=True)
    own_s = jnp.sum(squares[:, tl:], axis=1, keepdims=True)
    inv_t = lax.rsqrt(own_t / (tl * RZ) + EPS)
    inv_s = lax.rsqrt(own_s / ds + EPS)
    ibuf[p] = jnp.where(lane == 0, inv_t, inv_s)

    def i_copy(k):
        return remote(
            ibuf.at[p], ibuf.at[p], i_send.at[0], i_recv.at[0],
            at_plane((p + k) % PLANE),
        )

    @pl.loop(1, PLANE)
    def _(k):
        i_copy(k).start()

    r2.near()
    r2.column(0)
    r1.far()
    r1.column(-1)
    r1.column(1)
    r0.column(2)
    r3.middle()
    r2.far()
    r2.column(-1)
    r2.column(1)
    r1.column(2)
    await_recv(ibuf.at[pl.ds(0, PLANE - 1)], i_recv.at[0])
    for copy in l_copies:
        copy.wait()
    for copy in w_copies:
        copy.wait()

    all_t = ibuf[:, :, 0:1].reshape(PLANE * 8, 1)
    all_s = ibuf[:, :, 1:2].reshape(PLANE * 8, 1)

    def multiply(ring):
        pieces = [
            buf[ring.q, :, j].astype(F32).reshape(PLANE * 8, tl + sl) for j in range(4)
        ]
        cut_t = pl.ds(pl.multiple_of(ring.q * (4 * tl), 128), 4 * tl)
        cut_s = pl.ds(pl.multiple_of(ring.q * (4 * sl), 128), 4 * sl)
        v_t = jnp.concatenate([v[:, :tl] for v in pieces], axis=1)
        v_s = jnp.concatenate([v[:, tl:] for v in pieces], axis=1)
        x_t = (v_t * all_t * gt[:, cut_t]).astype(BF16)
        x_s = (v_s * all_s * gs[:, cut_s]).astype(BF16)
        d_t = lax.dot_general(wt[:, cut_t], x_t, NT, preferred_element_type=F32)
        d_s = lax.dot_general(ws[:, cut_s], x_s, NT, preferred_element_type=F32)
        if ring.c == 0:
            raw_t[...] = d_t
            raw_s[...] = d_s
        else:
            raw_t[...] += d_t
            raw_s[...] += d_s

    r0.finish()
    multiply(r0)
    r2.column(2)
    r1.finish()
    multiply(r1)
    r2.finish()
    r3.finish()
    multiply(r2)
    multiply(r3)

    sums = [jnp.zeros((1, 128), F32) for _ in range(7)]
    for half in range(2):
        vocab0 = ((p * 2 + half) * RZ + z) * vloc
        ids = vocab0 + lax.broadcasted_iota(jnp.int32, (vloc, 128), 0)
        onehot = ids == labels
        part = slice(half * vloc, (half + 1) * vloc)
        rs = raw_s[part]
        tan_t = jnp.tanh(raw_t[part] * (1.0 / CAP))
        tan_s = jnp.tanh(rs * (1.0 / CAP))
        log_t = CAP * tan_t
        log_s = CAP * tan_s
        exp_t = jnp.exp(log_t)
        exp_s = jnp.exp(log_s)
        slope = 1.0 - tan_s * tan_s
        e_s = exp_s * slope
        e_t = exp_t * slope
        o_h = jnp.where(onehot, slope, 0.0)
        es_s[half] = e_s
        et_s[half] = e_t
        oh_s[half] = o_h
        terms = (
            exp_t, exp_s, exp_t * (log_t - log_s), jnp.where(onehot, log_s, 0.0),
            e_s * rs, e_t * rs, o_h * rs,
        )
        sums = [a + jnp.sum(v, axis=0, keepdims=True) for a, v in zip(sums, terms)]

    sxy[p] = jnp.concatenate(sums + [jnp.zeros((1, 128), F32)], axis=0)

    def a_copy(k):
        return remote(
            sxy.at[p], sxy.at[p], a_send.at[0], a_recv.at[0],
            at_plane((p + k) % PLANE),
        )

    def b_copy(k):
        return remote(
            sz.at[z], sz.at[z], b_send.at[0], b_recv.at[0],
            at_line((z + k) % RZ),
        )

    @pl.loop(1, PLANE)
    def _(k):
        a_copy(k).start()

    await_recv(sxy.at[pl.ds(0, PLANE - 1)], a_recv.at[0])

    sz[z] = jnp.sum(sxy[...], axis=0)

    @pl.loop(1, RZ)
    def _(k):
        b_copy(k).start()

    await_recv(sz.at[pl.ds(0, RZ - 1)], b_recv.at[0])

    total = jnp.sum(sz[...], axis=0)
    sum_t, sum_s, cross, picked = (total[i : i + 1] for i in range(4))
    scale_s = 2.0 / sum_s
    scale_t = 1.0 / sum_t

    for half in range(2):
        grad = es_s[half] * scale_s - et_s[half] * scale_t - oh_s[half]
        gbuf[:, half * vloc : (half + 1) * vloc] = grad.T.astype(BF16)
    dh = ds // PARTS

    def r_copy(h, k):
        to = (p + k) % PLANE
        return remote(
            obuf.at[h, to], rbuf.at[h, p], r_send.at[h], r_recv.at[h], at_plane(to)
        )

    for h in range(PARTS):
        term = jnp.dot(
            gbuf[...], ws[:, h * dh : (h + 1) * dh], preferred_element_type=F32
        )
        obuf[h] = term.reshape(PLANE, 8, dh).astype(BF16)

        @pl.loop(1, PLANE)
        def _(k):
            r_copy(h, k).start()

    loss = cross / sum_t - jnp.log(sum_t) + 2.0 * jnp.log(sum_s) - picked
    radial = scale_s * total[4:5] - scale_t * total[5:6] - total[6:7]
    packed = jnp.concatenate([loss, radial, jnp.zeros((6, 128), F32)], axis=0)
    cols[...] = packed.T
    mine = cols[pl.ds(p * 8, 8), :]
    out_ref[:, 256:] = pltpu.roll(packed, (128 - p * 8) % 128, 1)
    rad = mine[:, 1:2]

    for h in range(PARTS):
        rbuf[h, p] = obuf[h, p]

    def q_start(h, k):
        to = h * (RZ // PARTS) + (z + k) % (RZ // PARTS)

        @pl.when(to != z)
        def _():
            remote(
                zsend.at[to], zrecv.at[z], q_send.at[0], q_recv.at[0], at_line(to)
            ).start()

    for h in range(PARTS):
        await_recv(rbuf.at[h, pl.ds(0, PLANE - 1)], r_recv.at[h])
        back = jnp.sum(rbuf[h].astype(F32), axis=0) * gs[:, h * dh : (h + 1) * dh]
        for k in range(RZ // PARTS):
            zsend[h * (RZ // PARTS) + k, :, :sl] = back[:, k * sl : (k + 1) * sl].astype(BF16)

        @pl.loop(0, RZ // PARTS)
        def _(k):
            q_start(h, k)

    await_send(buf.at[0, pl.ds(0, RZ - 1), 0], z_send.at[0])
    await_send(ibuf.at[pl.ds(0, PLANE - 1)], i_send.at[0])
    await_send(sxy.at[pl.ds(0, PLANE - 1)], a_send.at[0])
    await_send(sz.at[pl.ds(0, RZ - 1)], b_send.at[0])
    for ring in rings:
        await_send(buf.at[ring.q, pl.ds(0, 15)], g_send.at[ring.c])

    zrecv[z] = zsend[z]

    await_recv(zrecv.at[pl.ds(0, RZ - 1)], q_recv.at[0])

    sum_back = jnp.sum(zrecv[...].astype(F32), axis=0)[:, :sl]
    out = inv_s * sum_back - (inv_s * inv_s * rad) * sh_ref[...].astype(F32) / ds
    out_ref[:, :sl] = out

    for h in range(PARTS):
        await_send(obuf.at[h, pl.ds(0, PLANE - 1)], r_send.at[h])
    await_send(zsend.at[pl.ds(0, RZ - 1)], q_send.at[0])


def unpack(out_ref, loss_ref, grad_ref):
    loss_ref[...] = out_ref[0, 256 : 256 + loss_ref.shape[0]]
    grad_ref[...] = out_ref[:, : grad_ref.shape[1]].astype(BF16)


def on_device(th, sh, tg, sg, wt, ws, labels):
    tok, tl = th.shape
    sl = sh.shape[1]
    dt, ds, vloc = tl * RZ, sl * RZ, wt.shape[0]
    vmem = pl.BlockSpec(memory_space=pltpu.VMEM)
    hbm = pl.BlockSpec(memory_space=pl.ANY)
    dma = pltpu.SemaphoreType.DMA
    out = pl.pallas_call(
        kernel,
        out_shape=pltpu.VMEM((tok, 384), F32),
        in_specs=[hbm] * 7,
        out_specs=vmem,
        scratch_shapes=[
            pltpu.VMEM((tok, tl), BF16),
            pltpu.VMEM((tok, sl), BF16),
            pltpu.VMEM((dt // 128, 128), BF16),
            pltpu.VMEM((ds // 128, 128), BF16),
            pltpu.VMEM((2, 128), jnp.int32),
            pltpu.VMEM((2 * vloc, dt), BF16),
            pltpu.VMEM((2 * vloc, ds), BF16),
            pltpu.VMEM((4, PLANE, 4, tok, tl + sl), BF16),
            pltpu.VMEM((PLANE, tok, 128), F32),
            pltpu.VMEM((1, dt), F32),
            pltpu.VMEM((1, ds), F32),
            pltpu.VMEM((2 * vloc, 128), F32),
            pltpu.VMEM((2 * vloc, 128), F32),
            pltpu.VMEM((2, vloc, 128), F32),
            pltpu.VMEM((2, vloc, 128), F32),
            pltpu.VMEM((2, vloc, 128), F32),
            pltpu.VMEM((PLANE, 8, 128), F32),
            pltpu.VMEM((RZ, 8, 128), F32),
            pltpu.VMEM((128, 2 * vloc), BF16),
            pltpu.VMEM((PARTS, PLANE, tok, ds // PARTS), BF16),
            pltpu.VMEM((PARTS, PLANE, tok, ds // PARTS), BF16),
            pltpu.VMEM((RZ, tok, 256), BF16),
            pltpu.VMEM((RZ, tok, 256), BF16),
            pltpu.VMEM((128, 8), F32),
            dma((2,)), dma((2,)), dma((2,)), dma((5,)),
            dma((1,)), dma((4,)),
            dma((4,)), dma((4, 8)),
            dma((1,)), dma((1,)),
            dma((1,)), dma((1,)),
            dma((1,)), dma((1,)),
            dma((PARTS,)), dma((PARTS,)),
            dma((1,)), dma((1,)),
        ],
        compiler_params=pltpu.CompilerParams(
            collective_id=0, has_side_effects=True, vmem_limit_bytes=56 * 1024 * 1024
        ),
    )(th, sh, tg.reshape(-1, 128), sg.reshape(-1, 128), labels.reshape(2, 128), wt, ws)
    return pl.pallas_call(
        unpack,
        out_shape=(
            jax.ShapeDtypeStruct((tok,), F32), jax.ShapeDtypeStruct((tok, sl), BF16)
        ),
        in_specs=[vmem],
        out_specs=(vmem, vmem),
    )(pltpu.with_memory_space_constraint(out, pltpu.VMEM))


def solution(mesh):
    in_specs = (
        P("dp", ("group", "tensor")),
        P("dp", ("group", "tensor")),
        P(),
        P(),
        P(("dp", "group", "tensor"), None),
        P(("dp", "group", "tensor"), None),
        P(),
    )
    out_specs = (P("dp"), P("dp", ("group", "tensor")))
    return jax.shard_map(
        on_device, mesh=mesh, in_specs=in_specs, out_specs=out_specs, check_vma=False
    )
```

```python
import jax
import jax.numpy as jnp
from jax import lax
from jax.experimental import pallas as pl
from jax.experimental.pallas import tpu as pltpu
from jax.sharding import PartitionSpec as P

CAP = 30.0
EPS = 1e-06
MESH = pl.DeviceIdType.MESH
F32 = jnp.float32
BF16 = jnp.bfloat16
PARTS = 4
RX, RY, RZ = 4, 4, 16
PLANE = RX * RY
NT = (((1,), (1,)), ((), ()))


def kernel(
    th_hbm, sh_hbm, tg_hbm, sg_hbm, lab_hbm, wt_hbm, ws_hbm,
    out_ref,
    th_ref, sh_ref, tg_ref, sg_ref, lab_ref, wt, ws, buf, ibuf, gt, gs, raw_t, raw_s, es_s, et_s, oh_s,
    sxy, sz, gbuf, obuf, rbuf, zsend, zrecv, cols,
    w_send, w_recv, w_loc, s_loc, z_send, z_recv, g_send, g_recv, i_send, i_recv,
    a_send, a_recv, b_send, b_recv, r_send, r_recv, q_send, q_recv,
):
    dp = lax.axis_index("dp")
    z = lax.axis_index("group") * 8 + lax.axis_index("tensor")
    core = dp % 2
    p = dp // 2
    x = p % RX
    y = p // RX
    quad = z // 4
    tl = th_ref.shape[1]
    sl = sh_ref.shape[1]
    ds = sl * RZ
    vloc = wt_hbm.shape[0]

    def at_plane(q):
        return (q * 2 + core, lax.axis_index("group"), lax.axis_index("tensor"))

    def at_line(k):
        return (dp, k // 8, k % 8)

    my_rows = pl.ds(pl.multiple_of(core * vloc, vloc), vloc)
    partner = (p * 2 + 1 - core, lax.axis_index("group"), lax.axis_index("tensor"))

    def remote(src, dst, send, recv, device):
        return pltpu.make_async_remote_copy(
            src_ref=src, dst_ref=dst, send_sem=send, recv_sem=recv,
            device_id=device, device_id_type=MESH,
        )

    small = [
        pltpu.make_async_copy(src, dst, s_loc.at[i])
        for i, (src, dst) in enumerate(
            (
                (th_hbm, th_ref), (sh_hbm, sh_ref), (tg_hbm, tg_ref),
                (sg_hbm, sg_ref), (lab_hbm, lab_ref),
            )
        )
    ]
    for copy in small:
        copy.start()

    barrier = pltpu.get_barrier_semaphore()

    @pl.loop(1, RZ)
    def _(k):
        pl.semaphore_signal(
            barrier, inc=1, device_id=at_line((z + k) % RZ), device_id_type=MESH
        )
        pl.semaphore_signal(
            barrier, inc=1, device_id=at_plane((p + k) % PLANE), device_id_type=MESH
        )

    pl.semaphore_signal(barrier, inc=1, device_id=partner, device_id_type=MESH)

    l_copies = [
        pltpu.make_async_copy(wt_hbm, wt.at[my_rows], w_loc.at[0]),
        pltpu.make_async_copy(ws_hbm, ws.at[my_rows], w_loc.at[1]),
    ]
    for copy in l_copies:
        copy.start()

    for copy in small:
        copy.wait()

    own = jnp.concatenate(
        [th_ref[...].astype(F32), sh_ref[...].astype(F32)], axis=1
    )
    buf[quad, p, z % 4] = own.astype(BF16)

    for gain_ref, wide in ((tg_ref, gt), (sg_ref, gs)):
        gain = gain_ref[...].astype(F32)
        for i in range(gain.shape[0]):
            wide[:, i * 128 : (i + 1) * 128] = gain[i : i + 1]

    lane = lax.broadcasted_iota(jnp.int32, (8, 128), 1)
    label_row = jnp.zeros((8, 128), jnp.int32)
    for q in range(PLANE):
        row = jnp.broadcast_to(lab_ref[q // 8 : q // 8 + 1, :], (8, 128))
        shift = (8 * q - 16 * (q % 8) - 8 * core + 256) % 128
        label_row = jnp.where(lane // 8 == q, pltpu.roll(row, shift, 1), label_row)
    labels = label_row[:1, :]

    pl.semaphore_wait(barrier, 31)

    def await_recv(ref, sem):
        remote(ref, ref, w_send.at[0], sem, partner).wait_recv()

    def await_send(ref, sem):
        remote(ref, ref, sem, w_recv.at[0], partner).wait_send()

    slab = buf.at[quad, p, z % 4]

    def z_start(k):
        to = (z + k + RZ) % RZ
        remote(
            slab, slab, z_send.at[0], z_recv.at[(quad - to // 4 + 4) % 4], at_line(to)
        ).start()

    @pl.loop(1, 8)
    def _(k):
        z_start(k)
        z_start(-k)

    z_start(8)

    w_copies = [
        remote(wt_hbm, wt.at[my_rows], w_send.at[0], w_recv.at[0], partner),
        remote(ws_hbm, ws.at[my_rows], w_send.at[1], w_recv.at[1], partner),
    ]
    for copy in w_copies:
        copy.start()

    class Ring:
        def __init__(self, c, delta, x_first, way):
            self.c, self.q, self.delta = c, (quad + delta) % 4, delta
            self.x_first, self.way = x_first, way
            self.me1, self.me2 = (x, y) if x_first else (y, x)
            self.alone = {
                ("first", 1): 0, ("first", -1): 1, ("far", 0): 2,
                ("second", 0): 3, ("second", -1): 4, ("second", 1): 5, ("second", 2): 6,
            }

        def src(self, o1, o2):
            i1, i2 = (self.me1 + o1 + 4) % 4, (self.me2 + o2 + 4) % 4
            return i2 * RX + i1 if self.x_first else i1 * RX + i2

        def send(self, o1, o2, to1, to2, sem):
            ref = buf.at[self.q, self.src(o1, o2)]
            remote(
                ref, ref, g_send.at[self.c], g_recv.at[self.c, sem],
                at_plane(self.src(to1, to2)),
            ).start()

        def wait(self, sem):
            await_recv(buf.at[self.q, p], g_recv.at[self.c, sem])

        def second(self, o):
            self.send(o, 0, 0, self.way, self.alone["second", o])
            self.send(o, 0, 0, -self.way, 7)

        def begin(self):
            n = 3 if self.c == 0 else 4
            await_recv(buf.at[self.q, p, pl.ds(0, n)], z_recv.at[self.delta])
            for to in (1, -1):
                self.send(0, 0, to, 0, self.alone["first", to])
            self.second(0)

        def near(self):
            way = self.way
            self.wait(self.alone["first", way])
            self.send(-way, 0, way, 0, self.alone["far", 0])
            self.second(-way)
            self.wait(self.alone["first", -way])
            self.second(way)

        def far(self):
            self.wait(self.alone["far", 0])
            self.second(2)

        def column(self, o):
            self.wait(self.alone["second", o])
            self.send(o, -self.way, 0, self.way, 7)

        def finish(self):
            await_recv(buf.at[self.q, pl.ds(0, 8)], g_recv.at[self.c, 7])

    class TwoStep(Ring):
        def begin(self):
            await_recv(buf.at[self.q, p], z_recv.at[self.delta])
            for sem, to in enumerate((1, -1, 2)):
                self.send(0, 0, to, 0, sem)
            for to in (1, -1, 2):
                self.send(0, 0, 0, to, 7)

        def middle(self):
            for sem, o in enumerate((-1, 1, 2)):
                self.wait(sem)
                for to in (1, -1, 2):
                    self.send(o, 0, 0, to, 7)

        def finish(self):
            await_recv(buf.at[self.q, pl.ds(0, 12)], g_recv.at[self.c, 7])


    class TwoStep(Ring):
        def begin(self):
            await_recv(buf.at[self.q, p], z_recv.at[self.delta])
            for sem, to in enumerate((1, -1, 2)):
                self.send(0, 0, to, 0, sem)
            for to in (1, -1, 2):
                self.send(0, 0, 0, to, 7)

        def middle(self):
            for sem, o in enumerate((-1, 1, 2)):
                self.wait(sem)
                for to in (1, -1, 2):
                    self.send(o, 0, 0, to, 7)

        def finish(self):
            await_recv(buf.at[self.q, pl.ds(0, 12)], g_recv.at[self.c, 7])

    beside = jnp.where(z % 4 < 2, 3, 1)
    r0, r1, r2, r3 = rings = [
        Ring(0, 0, True, 1), Ring(1, beside, False, 1),
        Ring(2, 4 - beside, True, -1), TwoStep(3, 2, False, -1),
    ]
    r0.begin()
    r1.begin()
    r0.near()
    r0.column(0)
    r2.begin()
    r3.begin()
    r1.near()
    r1.column(0)
    r0.far()
    r0.column(-1)
    r0.column(1)
    squares = jnp.zeros((8, tl + sl), F32)
    for k in range(4):
        for j in range(4):
            v = buf[k, p, j].astype(F32)
            squares = squares + v * v
    own_t = jnp.sum(squares[:, :tl], axis=1, keepdims=True)
    own_s = jnp.sum(squares[:, tl:], axis=1, keepdims=True)
    inv_t = lax.rsqrt(own_t / (tl * RZ) + EPS)
    inv_s = lax.rsqrt(own_s / ds + EPS)
    ibuf[p] = jnp.where(lane == 0, inv_t, inv_s)

    def i_copy(k):
        return remote(
            ibuf.at[p], ibuf.at[p], i_send.at[0], i_recv.at[0],
            at_plane((p + k) % PLANE),
        )

    @pl.loop(1, PLANE)
    def _(k):
        i_copy(k).start()

    r2.near()
    r2.column(0)
    r1.far()
    r1.column(-1)
    r1.column(1)
    r0.column(2)
    r3.middle()
    r2.far()
    r2.column(-1)
    r2.column(1)
    r1.column(2)
    await_recv(ibuf.at[pl.ds(0, PLANE - 1)], i_recv.at[0])
    for copy in l_copies:
        copy.wait()
    for copy in w_copies:
        copy.wait()

    all_t = ibuf[:, :, 0:1].reshape(PLANE * 8, 1)
    all_s = ibuf[:, :, 1:2].reshape(PLANE * 8, 1)

    def multiply(ring):
        pieces = [
            buf[ring.q, :, j].astype(F32).reshape(PLANE * 8, tl + sl) for j in range(4)
        ]
        cut_t = pl.ds(pl.multiple_of(ring.q * (4 * tl), 128), 4 * tl)
        cut_s = pl.ds(pl.multiple_of(ring.q * (4 * sl), 128), 4 * sl)
        v_t = jnp.concatenate([v[:, :tl] for v in pieces], axis=1)
        v_s = jnp.concatenate([v[:, tl:] for v in pieces], axis=1)
        x_t = (v_t * all_t * gt[:, cut_t]).astype(BF16)
        x_s = (v_s * all_s * gs[:, cut_s]).astype(BF16)
        d_t = lax.dot_general(wt[:, cut_t], x_t, NT, preferred_element_type=F32)
        d_s = lax.dot_general(ws[:, cut_s], x_s, NT, preferred_element_type=F32)
        if ring.c == 0:
            raw_t[...] = d_t
            raw_s[...] = d_s
        else:
            raw_t[...] += d_t
            raw_s[...] += d_s

    r0.finish()
    multiply(r0)
    r2.column(2)
    r1.finish()
    multiply(r1)
    r2.finish()
    r3.finish()
    multiply(r2)
    multiply(r3)

    sums = [jnp.zeros((1, 128), F32) for _ in range(7)]
    for half in range(2):
        vocab0 = ((p * 2 + half) * RZ + z) * vloc
        ids = vocab0 + lax.broadcasted_iota(jnp.int32, (vloc, 128), 0)
        onehot = ids == labels
        part = slice(half * vloc, (half + 1) * vloc)
        rs = raw_s[part]
        tan_t = jnp.tanh(raw_t[part] * (1.0 / CAP))
        tan_s = jnp.tanh(rs * (1.0 / CAP))
        log_t = CAP * tan_t
        log_s = CAP * tan_s
        exp_t = jnp.exp(log_t)
        exp_s = jnp.exp(log_s)
        slope = 1.0 - tan_s * tan_s
        e_s = exp_s * slope
        e_t = exp_t * slope
        o_h = jnp.where(onehot, slope, 0.0)
        es_s[half] = e_s
        et_s[half] = e_t
        oh_s[half] = o_h
        terms = (
            exp_t, exp_s, exp_t * (log_t - log_s), jnp.where(onehot, log_s, 0.0),
            e_s * rs, e_t * rs, o_h * rs,
        )
        sums = [a + jnp.sum(v, axis=0, keepdims=True) for a, v in zip(sums, terms)]

    sxy[p] = jnp.concatenate(sums + [jnp.zeros((1, 128), F32)], axis=0)

    def a_copy(k):
        return remote(
            sxy.at[p], sxy.at[p], a_send.at[0], a_recv.at[0],
            at_plane((p + k) % PLANE),
        )

    def b_copy(k):
        return remote(
            sz.at[z], sz.at[z], b_send.at[0], b_recv.at[0],
            at_line((z + k) % RZ),
        )

    @pl.loop(1, PLANE)
    def _(k):
        a_copy(k).start()

    await_recv(sxy.at[pl.ds(0, PLANE - 1)], a_recv.at[0])

    sz[z] = jnp.sum(sxy[...], axis=0)

    for k in (8, 7, 9, 6, 10, 5, 11, 4, 12, 3, 13, 2, 14, 1, 15):
        b_copy(k).start()

    await_recv(sz.at[pl.ds(0, RZ - 1)], b_recv.at[0])

    total = jnp.sum(sz[...], axis=0)
    sum_t, sum_s, cross, picked = (total[i : i + 1] for i in range(4))
    scale_s = 2.0 / sum_s
    scale_t = 1.0 / sum_t

    for half in range(2):
        grad = es_s[half] * scale_s - et_s[half] * scale_t - oh_s[half]
        gbuf[:, half * vloc : (half + 1) * vloc] = grad.T.astype(BF16)
    dh = ds // PARTS

    def r_copy(h, k):
        to = (p + k) % PLANE
        return remote(
            obuf.at[h, to], rbuf.at[h, p], r_send.at[h], r_recv.at[h], at_plane(to)
        )

    for h in range(PARTS):
        term = jnp.dot(
            gbuf[...], ws[:, h * dh : (h + 1) * dh], preferred_element_type=F32
        )
        obuf[h] = term.reshape(PLANE, 8, dh).astype(BF16)

        @pl.loop(1, PLANE)
        def _(k):
            r_copy(h, k).start()

    loss = cross / sum_t - jnp.log(sum_t) + 2.0 * jnp.log(sum_s) - picked
    radial = scale_s * total[4:5] - scale_t * total[5:6] - total[6:7]
    packed = jnp.concatenate([loss, radial, jnp.zeros((6, 128), F32)], axis=0)
    cols[...] = packed.T
    mine = cols[pl.ds(p * 8, 8), :]
    out_ref[:, 256:] = pltpu.roll(packed, (128 - p * 8) % 128, 1)
    rad = mine[:, 1:2]

    for h in range(PARTS):
        rbuf[h, p] = obuf[h, p]

    def q_start(h, k):
        to = h * (RZ // PARTS) + (z + k) % (RZ // PARTS)

        @pl.when(to != z)
        def _():
            remote(
                zsend.at[to], zrecv.at[z], q_send.at[0], q_recv.at[0], at_line(to)
            ).start()

    for h in range(PARTS):
        await_recv(rbuf.at[h, pl.ds(0, PLANE - 1)], r_recv.at[h])
        back = jnp.sum(rbuf[h].astype(F32), axis=0) * gs[:, h * dh : (h + 1) * dh]
        for k in range(RZ // PARTS):
            zsend[h * (RZ // PARTS) + k, :, :sl] = back[:, k * sl : (k + 1) * sl].astype(BF16)

        @pl.loop(0, RZ // PARTS)
        def _(k):
            q_start(h, k)

    await_send(buf.at[0, pl.ds(0, RZ - 1), 0], z_send.at[0])
    await_send(ibuf.at[pl.ds(0, PLANE - 1)], i_send.at[0])
    await_send(sxy.at[pl.ds(0, PLANE - 1)], a_send.at[0])
    await_send(sz.at[pl.ds(0, RZ - 1)], b_send.at[0])
    for ring in rings:
        await_send(buf.at[ring.q, pl.ds(0, 15)], g_send.at[ring.c])

    zrecv[z] = zsend[z]

    await_recv(zrecv.at[pl.ds(0, RZ - 1)], q_recv.at[0])

    sum_back = jnp.sum(zrecv[...].astype(F32), axis=0)[:, :sl]
    out = inv_s * sum_back - (inv_s * inv_s * rad) * sh_ref[...].astype(F32) / ds
    out_ref[:, :sl] = out

    for h in range(PARTS):
        await_send(obuf.at[h, pl.ds(0, PLANE - 1)], r_send.at[h])
    await_send(zsend.at[pl.ds(0, RZ - 1)], q_send.at[0])


def unpack(out_ref, loss_ref, grad_ref):
    loss_ref[...] = out_ref[0, 256 : 256 + loss_ref.shape[0]]
    grad_ref[...] = out_ref[:, : grad_ref.shape[1]].astype(BF16)


def on_device(th, sh, tg, sg, wt, ws, labels):
    tok, tl = th.shape
    sl = sh.shape[1]
    dt, ds, vloc = tl * RZ, sl * RZ, wt.shape[0]
    vmem = pl.BlockSpec(memory_space=pltpu.VMEM)
    hbm = pl.BlockSpec(memory_space=pl.ANY)
    dma = pltpu.SemaphoreType.DMA
    out = pl.pallas_call(
        kernel,
        out_shape=pltpu.VMEM((tok, 384), F32),
        in_specs=[hbm] * 7,
        out_specs=vmem,
        scratch_shapes=[
            pltpu.VMEM((tok, tl), BF16),
            pltpu.VMEM((tok, sl), BF16),
            pltpu.VMEM((dt // 128, 128), BF16),
            pltpu.VMEM((ds // 128, 128), BF16),
            pltpu.VMEM((2, 128), jnp.int32),
            pltpu.VMEM((2 * vloc, dt), BF16),
            pltpu.VMEM((2 * vloc, ds), BF16),
            pltpu.VMEM((4, PLANE, 4, tok, tl + sl), BF16),
            pltpu.VMEM((PLANE, tok, 128), F32),
            pltpu.VMEM((1, dt), F32),
            pltpu.VMEM((1, ds), F32),
            pltpu.VMEM((2 * vloc, 128), F32),
            pltpu.VMEM((2 * vloc, 128), F32),
            pltpu.VMEM((2, vloc, 128), F32),
            pltpu.VMEM((2, vloc, 128), F32),
            pltpu.VMEM((2, vloc, 128), F32),
            pltpu.VMEM((PLANE, 8, 128), F32),
            pltpu.VMEM((RZ, 8, 128), F32),
            pltpu.VMEM((128, 2 * vloc), BF16),
            pltpu.VMEM((PARTS, PLANE, tok, ds // PARTS), BF16),
            pltpu.VMEM((PARTS, PLANE, tok, ds // PARTS), BF16),
            pltpu.VMEM((RZ, tok, 256), BF16),
            pltpu.VMEM((RZ, tok, 256), BF16),
            pltpu.VMEM((128, 8), F32),
            dma((2,)), dma((2,)), dma((2,)), dma((5,)),
            dma((1,)), dma((4,)),
            dma((4,)), dma((4, 8)),
            dma((1,)), dma((1,)),
            dma((1,)), dma((1,)),
            dma((1,)), dma((1,)),
            dma((PARTS,)), dma((PARTS,)),
            dma((1,)), dma((1,)),
        ],
        compiler_params=pltpu.CompilerParams(
            collective_id=0, has_side_effects=True, vmem_limit_bytes=56 * 1024 * 1024
        ),
    )(th, sh, tg.reshape(-1, 128), sg.reshape(-1, 128), labels.reshape(2, 128), wt, ws)
    return pl.pallas_call(
        unpack,
        out_shape=(
            jax.ShapeDtypeStruct((tok,), F32), jax.ShapeDtypeStruct((tok, sl), BF16)
        ),
        in_specs=[vmem],
        out_specs=(vmem, vmem),
    )(pltpu.with_memory_space_constraint(out, pltpu.VMEM))


def solution(mesh):
    in_specs = (
        P("dp", ("group", "tensor")),
        P("dp", ("group", "tensor")),
        P(),
        P(),
        P(("dp", "group", "tensor"), None),
        P(("dp", "group", "tensor"), None),
        P(),
    )
    out_specs = (P("dp"), P("dp", ("group", "tensor")))
    return jax.shard_map(
        on_device, mesh=mesh, in_specs=in_specs, out_specs=out_specs, check_vma=False
    )
```

```python
import jax
import jax.numpy as jnp
from jax import lax
from jax.experimental import pallas as pl
from jax.experimental.pallas import tpu as pltpu
from jax.sharding import PartitionSpec as P

CAP = 30.0
EPS = 1e-06
MESH = pl.DeviceIdType.MESH
F32 = jnp.float32
BF16 = jnp.bfloat16
PARTS = 4
RX, RY, RZ = 4, 4, 16
PLANE = RX * RY
NT = (((1,), (1,)), ((), ()))


def kernel(
    th_hbm, sh_hbm, tg_hbm, sg_hbm, lab_hbm, wt_hbm, ws_hbm,
    out_ref,
    th_ref, sh_ref, tg_ref, sg_ref, lab_ref, wt, ws, buf, ibuf, gt, gs, raw_t, raw_s, es_s, et_s, oh_s,
    sxy, sz, gbuf, obuf, rbuf, zsend, zrecv, cols,
    w_send, w_recv, w_loc, s_loc, z_send, z_recv, g_send, g_recv, i_send, i_recv,
    a_send, a_recv, b_send, b_recv, r_send, r_recv, q_send, q_recv,
):
    dp = lax.axis_index("dp")
    z = lax.axis_index("group") * 8 + lax.axis_index("tensor")
    core = dp % 2
    p = dp // 2
    x = p % RX
    y = p // RX
    quad = z // 4
    tl = th_ref.shape[1]
    sl = sh_ref.shape[1]
    ds = sl * RZ
    vloc = wt_hbm.shape[0]

    def at_plane(q):
        return (q * 2 + core, lax.axis_index("group"), lax.axis_index("tensor"))

    def at_line(k):
        return (dp, k // 8, k % 8)

    my_rows = pl.ds(pl.multiple_of(core * vloc, vloc), vloc)
    partner = (p * 2 + 1 - core, lax.axis_index("group"), lax.axis_index("tensor"))

    def remote(src, dst, send, recv, device):
        return pltpu.make_async_remote_copy(
            src_ref=src, dst_ref=dst, send_sem=send, recv_sem=recv,
            device_id=device, device_id_type=MESH,
        )

    small = [
        pltpu.make_async_copy(src, dst, s_loc.at[i])
        for i, (src, dst) in enumerate(
            (
                (th_hbm, th_ref), (sh_hbm, sh_ref), (tg_hbm, tg_ref),
                (sg_hbm, sg_ref), (lab_hbm, lab_ref),
            )
        )
    ]
    for copy in small:
        copy.start()

    barrier = pltpu.get_barrier_semaphore()

    @pl.loop(1, RZ)
    def _(k):
        pl.semaphore_signal(
            barrier, inc=1, device_id=at_line((z + k) % RZ), device_id_type=MESH
        )
        pl.semaphore_signal(
            barrier, inc=1, device_id=at_plane((p + k) % PLANE), device_id_type=MESH
        )

    pl.semaphore_signal(barrier, inc=1, device_id=partner, device_id_type=MESH)

    l_copies = [
        pltpu.make_async_copy(wt_hbm, wt.at[my_rows], w_loc.at[0]),
        pltpu.make_async_copy(ws_hbm, ws.at[my_rows], w_loc.at[1]),
    ]
    for copy in l_copies:
        copy.start()

    for copy in small:
        copy.wait()

    own = jnp.concatenate(
        [th_ref[...].astype(F32), sh_ref[...].astype(F32)], axis=1
    )
    buf[quad, p, z % 4] = own.astype(BF16)

    for gain_ref, wide in ((tg_ref, gt), (sg_ref, gs)):
        gain = gain_ref[...].astype(F32)
        for i in range(gain.shape[0]):
            wide[:, i * 128 : (i + 1) * 128] = gain[i : i + 1]

    lane = lax.broadcasted_iota(jnp.int32, (8, 128), 1)
    label_row = jnp.zeros((8, 128), jnp.int32)
    for q in range(PLANE):
        row = jnp.broadcast_to(lab_ref[q // 8 : q // 8 + 1, :], (8, 128))
        shift = (8 * q - 16 * (q % 8) - 8 * core + 256) % 128
        label_row = jnp.where(lane // 8 == q, pltpu.roll(row, shift, 1), label_row)
    labels = label_row[:1, :]

    pl.semaphore_wait(barrier, 31)

    def await_recv(ref, sem):
        remote(ref, ref, w_send.at[0], sem, partner).wait_recv()

    def await_send(ref, sem):
        remote(ref, ref, sem, w_recv.at[0], partner).wait_send()

    slab = buf.at[quad, p, z % 4]

    def z_start(k):
        to = (z + k + RZ) % RZ
        remote(
            slab, slab, z_send.at[0], z_recv.at[(quad - to // 4 + 4) % 4], at_line(to)
        ).start()

    @pl.loop(1, 8)
    def _(k):
        z_start(k)
        z_start(-k)

    z_start(8)

    w_copies = [
        remote(wt_hbm, wt.at[my_rows], w_send.at[0], w_recv.at[0], partner),
        remote(ws_hbm, ws.at[my_rows], w_send.at[1], w_recv.at[1], partner),
    ]
    class Ring:
        def __init__(self, c, delta, x_first, way):
            self.c, self.q, self.delta = c, (quad + delta) % 4, delta
            self.x_first, self.way = x_first, way
            self.me1, self.me2 = (x, y) if x_first else (y, x)
            self.alone = {
                ("first", 1): 0, ("first", -1): 1, ("far", 0): 2,
                ("second", 0): 3, ("second", -1): 4, ("second", 1): 5, ("second", 2): 6,
            }

        def src(self, o1, o2):
            i1, i2 = (self.me1 + o1 + 4) % 4, (self.me2 + o2 + 4) % 4
            return i2 * RX + i1 if self.x_first else i1 * RX + i2

        def send(self, o1, o2, to1, to2, sem):
            ref = buf.at[self.q, self.src(o1, o2)]
            remote(
                ref, ref, g_send.at[self.c], g_recv.at[self.c, sem],
                at_plane(self.src(to1, to2)),
            ).start()

        def wait(self, sem):
            await_recv(buf.at[self.q, p], g_recv.at[self.c, sem])

        def second(self, o):
            self.send(o, 0, 0, self.way, self.alone["second", o])
            self.send(o, 0, 0, -self.way, 7)

        def begin(self):
            n = 3 if self.c == 0 else 4
            await_recv(buf.at[self.q, p, pl.ds(0, n)], z_recv.at[self.delta])
            for to in (1, -1):
                self.send(0, 0, to, 0, self.alone["first", to])
            self.second(0)

        def near(self):
            way = self.way
            self.wait(self.alone["first", way])
            self.send(-way, 0, way, 0, self.alone["far", 0])
            self.second(-way)
            self.wait(self.alone["first", -way])
            self.second(way)

        def far(self):
            self.wait(self.alone["far", 0])
            self.second(2)

        def column(self, o):
            self.wait(self.alone["second", o])
            self.send(o, -self.way, 0, self.way, 7)

        def finish(self):
            await_recv(buf.at[self.q, pl.ds(0, 8)], g_recv.at[self.c, 7])

    class TwoStep(Ring):
        def begin(self):
            await_recv(buf.at[self.q, p], z_recv.at[self.delta])
            for sem, to in enumerate((1, -1, 2)):
                self.send(0, 0, to, 0, sem)
            for to in (1, -1, 2):
                self.send(0, 0, 0, to, 7)

        def middle(self):
            for sem, o in enumerate((-1, 1, 2)):
                self.wait(sem)
                for to in (1, -1, 2):
                    self.send(o, 0, 0, to, 7)

        def finish(self):
            await_recv(buf.at[self.q, pl.ds(0, 12)], g_recv.at[self.c, 7])


    class TwoStep(Ring):
        def begin(self):
            await_recv(buf.at[self.q, p], z_recv.at[self.delta])
            for sem, to in enumerate((1, -1, 2)):
                self.send(0, 0, to, 0, sem)
            for to in (1, -1, 2):
                self.send(0, 0, 0, to, 7)

        def middle(self):
            for sem, o in enumerate((-1, 1, 2)):
                self.wait(sem)
                for to in (1, -1, 2):
                    self.send(o, 0, 0, to, 7)

        def finish(self):
            await_recv(buf.at[self.q, pl.ds(0, 12)], g_recv.at[self.c, 7])

    beside = jnp.where(z % 4 < 2, 3, 1)
    r0, r1, r2, r3 = rings = [
        Ring(0, 0, True, 1), Ring(1, beside, False, 1),
        Ring(2, 4 - beside, True, -1), TwoStep(3, 2, False, -1),
    ]
    r0.begin()
    for copy in w_copies:
        copy.start()

    r1.begin()
    r0.near()
    r0.column(0)
    r2.begin()
    r3.begin()
    r1.near()
    r1.column(0)
    r0.far()
    r0.column(-1)
    r0.column(1)
    squares = jnp.zeros((8, tl + sl), F32)
    for k in range(4):
        for j in range(4):
            v = buf[k, p, j].astype(F32)
            squares = squares + v * v
    own_t = jnp.sum(squares[:, :tl], axis=1, keepdims=True)
    own_s = jnp.sum(squares[:, tl:], axis=1, keepdims=True)
    inv_t = lax.rsqrt(own_t / (tl * RZ) + EPS)
    inv_s = lax.rsqrt(own_s / ds + EPS)
    ibuf[p] = jnp.where(lane == 0, inv_t, inv_s)

    def i_copy(k):
        return remote(
            ibuf.at[p], ibuf.at[p], i_send.at[0], i_recv.at[0],
            at_plane((p + k) % PLANE),
        )

    @pl.loop(1, PLANE)
    def _(k):
        i_copy(k).start()

    r2.near()
    r2.column(0)
    r1.far()
    r1.column(-1)
    r1.column(1)
    r0.column(2)
    r3.middle()
    r2.far()
    r2.column(-1)
    r2.column(1)
    r1.column(2)
    await_recv(ibuf.at[pl.ds(0, PLANE - 1)], i_recv.at[0])
    for copy in l_copies:
        copy.wait()
    for copy in w_copies:
        copy.wait()

    all_t = ibuf[:, :, 0:1].reshape(PLANE * 8, 1)
    all_s = ibuf[:, :, 1:2].reshape(PLANE * 8, 1)

    def multiply(ring):
        pieces = [
            buf[ring.q, :, j].astype(F32).reshape(PLANE * 8, tl + sl) for j in range(4)
        ]
        cut_t = pl.ds(pl.multiple_of(ring.q * (4 * tl), 128), 4 * tl)
        cut_s = pl.ds(pl.multiple_of(ring.q * (4 * sl), 128), 4 * sl)
        v_t = jnp.concatenate([v[:, :tl] for v in pieces], axis=1)
        v_s = jnp.concatenate([v[:, tl:] for v in pieces], axis=1)
        x_t = (v_t * all_t * gt[:, cut_t]).astype(BF16)
        x_s = (v_s * all_s * gs[:, cut_s]).astype(BF16)
        d_t = lax.dot_general(wt[:, cut_t], x_t, NT, preferred_element_type=F32)
        d_s = lax.dot_general(ws[:, cut_s], x_s, NT, preferred_element_type=F32)
        if ring.c == 0:
            raw_t[...] = d_t
            raw_s[...] = d_s
        else:
            raw_t[...] += d_t
            raw_s[...] += d_s

    r0.finish()
    multiply(r0)
    r2.column(2)
    r1.finish()
    multiply(r1)
    r2.finish()
    r3.finish()
    multiply(r2)
    multiply(r3)

    sums = [jnp.zeros((1, 128), F32) for _ in range(7)]
    for half in range(2):
        vocab0 = ((p * 2 + half) * RZ + z) * vloc
        ids = vocab0 + lax.broadcasted_iota(jnp.int32, (vloc, 128), 0)
        onehot = ids == labels
        part = slice(half * vloc, (half + 1) * vloc)
        rs = raw_s[part]
        tan_t = jnp.tanh(raw_t[part] * (1.0 / CAP))
        tan_s = jnp.tanh(rs * (1.0 / CAP))
        log_t = CAP * tan_t
        log_s = CAP * tan_s
        exp_t = jnp.exp(log_t)
        exp_s = jnp.exp(log_s)
        slope = 1.0 - tan_s * tan_s
        e_s = exp_s * slope
        e_t = exp_t * slope
        o_h = jnp.where(onehot, slope, 0.0)
        es_s[half] = e_s
        et_s[half] = e_t
        oh_s[half] = o_h
        terms = (
            exp_t, exp_s, exp_t * (log_t - log_s), jnp.where(onehot, log_s, 0.0),
            e_s * rs, e_t * rs, o_h * rs,
        )
        sums = [a + jnp.sum(v, axis=0, keepdims=True) for a, v in zip(sums, terms)]

    sxy[p] = jnp.concatenate(sums + [jnp.zeros((1, 128), F32)], axis=0)

    def a_copy(k):
        return remote(
            sxy.at[p], sxy.at[p], a_send.at[0], a_recv.at[0],
            at_plane((p + k) % PLANE),
        )

    def b_copy(k):
        return remote(
            sz.at[z], sz.at[z], b_send.at[0], b_recv.at[0],
            at_line((z + k) % RZ),
        )

    @pl.loop(1, PLANE)
    def _(k):
        a_copy(k).start()

    await_recv(sxy.at[pl.ds(0, PLANE - 1)], a_recv.at[0])

    sz[z] = jnp.sum(sxy[...], axis=0)

    for k in (8, 7, 9, 6, 10, 5, 11, 4, 12, 3, 13, 2, 14, 1, 15):
        b_copy(k).start()

    await_recv(sz.at[pl.ds(0, RZ - 1)], b_recv.at[0])

    total = jnp.sum(sz[...], axis=0)
    sum_t, sum_s, cross, picked = (total[i : i + 1] for i in range(4))
    scale_s = 2.0 / sum_s
    scale_t = 1.0 / sum_t

    for half in range(2):
        grad = es_s[half] * scale_s - et_s[half] * scale_t - oh_s[half]
        gbuf[:, half * vloc : (half + 1) * vloc] = grad.T.astype(BF16)
    dh = ds // PARTS

    def r_copy(h, k):
        to = (p + k) % PLANE
        return remote(
            obuf.at[h, to], rbuf.at[h, p], r_send.at[h], r_recv.at[h], at_plane(to)
        )

    for h in range(PARTS):
        term = jnp.dot(
            gbuf[...], ws[:, h * dh : (h + 1) * dh], preferred_element_type=F32
        )
        obuf[h] = term.reshape(PLANE, 8, dh).astype(BF16)

        @pl.loop(1, PLANE)
        def _(k):
            r_copy(h, k).start()

    loss = cross / sum_t - jnp.log(sum_t) + 2.0 * jnp.log(sum_s) - picked
    radial = scale_s * total[4:5] - scale_t * total[5:6] - total[6:7]
    packed = jnp.concatenate([loss, radial, jnp.zeros((6, 128), F32)], axis=0)
    cols[...] = packed.T
    mine = cols[pl.ds(p * 8, 8), :]
    out_ref[:, 256:] = pltpu.roll(packed, (128 - p * 8) % 128, 1)
    rad = mine[:, 1:2]

    for h in range(PARTS):
        rbuf[h, p] = obuf[h, p]

    def q_start(h, k):
        to = h * (RZ // PARTS) + (z + k) % (RZ // PARTS)

        @pl.when(to != z)
        def _():
            remote(
                zsend.at[to], zrecv.at[z], q_send.at[0], q_recv.at[0], at_line(to)
            ).start()

    for h in range(PARTS):
        await_recv(rbuf.at[h, pl.ds(0, PLANE - 1)], r_recv.at[h])
        back = jnp.sum(rbuf[h].astype(F32), axis=0) * gs[:, h * dh : (h + 1) * dh]
        for k in range(RZ // PARTS):
            zsend[h * (RZ // PARTS) + k, :, :sl] = back[:, k * sl : (k + 1) * sl].astype(BF16)

        @pl.loop(0, RZ // PARTS)
        def _(k):
            q_start(h, k)

    await_send(buf.at[0, pl.ds(0, RZ - 1), 0], z_send.at[0])
    await_send(ibuf.at[pl.ds(0, PLANE - 1)], i_send.at[0])
    await_send(sxy.at[pl.ds(0, PLANE - 1)], a_send.at[0])
    await_send(sz.at[pl.ds(0, RZ - 1)], b_send.at[0])
    for ring in rings:
        await_send(buf.at[ring.q, pl.ds(0, 15)], g_send.at[ring.c])

    zrecv[z] = zsend[z]

    await_recv(zrecv.at[pl.ds(0, RZ - 1)], q_recv.at[0])

    sum_back = jnp.sum(zrecv[...].astype(F32), axis=0)[:, :sl]
    out = inv_s * sum_back - (inv_s * inv_s * rad) * sh_ref[...].astype(F32) / ds
    out_ref[:, :sl] = out

    for h in range(PARTS):
        await_send(obuf.at[h, pl.ds(0, PLANE - 1)], r_send.at[h])
    await_send(zsend.at[pl.ds(0, RZ - 1)], q_send.at[0])


def unpack(out_ref, loss_ref, grad_ref):
    loss_ref[...] = out_ref[0, 256 : 256 + loss_ref.shape[0]]
    grad_ref[...] = out_ref[:, : grad_ref.shape[1]].astype(BF16)


def on_device(th, sh, tg, sg, wt, ws, labels):
    tok, tl = th.shape
    sl = sh.shape[1]
    dt, ds, vloc = tl * RZ, sl * RZ, wt.shape[0]
    vmem = pl.BlockSpec(memory_space=pltpu.VMEM)
    hbm = pl.BlockSpec(memory_space=pl.ANY)
    dma = pltpu.SemaphoreType.DMA
    out = pl.pallas_call(
        kernel,
        out_shape=pltpu.VMEM((tok, 384), F32),
        in_specs=[hbm] * 7,
        out_specs=vmem,
        scratch_shapes=[
            pltpu.VMEM((tok, tl), BF16),
            pltpu.VMEM((tok, sl), BF16),
            pltpu.VMEM((dt // 128, 128), BF16),
            pltpu.VMEM((ds // 128, 128), BF16),
            pltpu.VMEM((2, 128), jnp.int32),
            pltpu.VMEM((2 * vloc, dt), BF16),
            pltpu.VMEM((2 * vloc, ds), BF16),
            pltpu.VMEM((4, PLANE, 4, tok, tl + sl), BF16),
            pltpu.VMEM((PLANE, tok, 128), F32),
            pltpu.VMEM((1, dt), F32),
            pltpu.VMEM((1, ds), F32),
            pltpu.VMEM((2 * vloc, 128), F32),
            pltpu.VMEM((2 * vloc, 128), F32),
            pltpu.VMEM((2, vloc, 128), F32),
            pltpu.VMEM((2, vloc, 128), F32),
            pltpu.VMEM((2, vloc, 128), F32),
            pltpu.VMEM((PLANE, 8, 128), F32),
            pltpu.VMEM((RZ, 8, 128), F32),
            pltpu.VMEM((128, 2 * vloc), BF16),
            pltpu.VMEM((PARTS, PLANE, tok, ds // PARTS), BF16),
            pltpu.VMEM((PARTS, PLANE, tok, ds // PARTS), BF16),
            pltpu.VMEM((RZ, tok, 256), BF16),
            pltpu.VMEM((RZ, tok, 256), BF16),
            pltpu.VMEM((128, 8), F32),
            dma((2,)), dma((2,)), dma((2,)), dma((5,)),
            dma((1,)), dma((4,)),
            dma((4,)), dma((4, 8)),
            dma((1,)), dma((1,)),
            dma((1,)), dma((1,)),
            dma((1,)), dma((1,)),
            dma((PARTS,)), dma((PARTS,)),
            dma((1,)), dma((1,)),
        ],
        compiler_params=pltpu.CompilerParams(
            collective_id=0, has_side_effects=True, vmem_limit_bytes=56 * 1024 * 1024
        ),
    )(th, sh, tg.reshape(-1, 128), sg.reshape(-1, 128), labels.reshape(2, 128), wt, ws)
    return pl.pallas_call(
        unpack,
        out_shape=(
            jax.ShapeDtypeStruct((tok,), F32), jax.ShapeDtypeStruct((tok, sl), BF16)
        ),
        in_specs=[vmem],
        out_specs=(vmem, vmem),
    )(pltpu.with_memory_space_constraint(out, pltpu.VMEM))


def solution(mesh):
    in_specs = (
        P("dp", ("group", "tensor")),
        P("dp", ("group", "tensor")),
        P(),
        P(),
        P(("dp", "group", "tensor"), None),
        P(("dp", "group", "tensor"), None),
        P(),
    )
    out_specs = (P("dp"), P("dp", ("group", "tensor")))
    return jax.shard_map(
        on_device, mesh=mesh, in_specs=in_specs, out_specs=out_specs, check_vma=False
    )
```
